32 devices in a mesh: blk: 8 (over z, y), rep: 4 (over x, core).
Axes of the slice: x: 2, y: 2, z: 4, core: 2. Of those that a mesh axis runs over, the one named last changes fastest.
Arguments:
- features: bfloat16 [8192, 256], P(('blk', 'rep')), may hold values from -6 to 6
- w_self: bfloat16 [256, 256], replicated, may hold values from -0.375 to 0.375
- w_neigh: bfloat16 [256, 256], replicated, may hold values from -0.375 to 0.375
- bias: float32 [256], replicated, may hold values from -3 to 3
- cotangent: bfloat16 [8192, 256], P(('blk', 'rep')), may hold values from -6 to 6
- tile_values: bfloat16 [8, 4, 8, 12, 128, 128], P('blk', 'rep')
- tile_rows: int32 [8, 4, 8, 12], P('blk', 'rep'), may hold values from 0 to 7, as said below
- tile_cols: int32 [8, 4, 8, 12], P('blk', 'rep'), may hold values from 0 to 1
- tile_counts: int32 [8, 4, 8], P('blk', 'rep'), may hold values from 1 to 12, as said below
Outputs:
- output: bfloat16 [8192, 256], P(('blk', 'rep'))
- grad_features: bfloat16 [8192, 256], P(('blk', 'rep'))
- grad_self: float32 [256, 256], replicated
- grad_neigh: float32 [256, 256], replicated
- grad_bias: float32 [256], replicated
The draws below stay inside these ranges and needn't reach their ends.
Inputs may be any that keep to these rules, and one draw needn't show every extreme that they name: Among the live slots s < tile_counts[b, r, c] of one b, r, c, the pairs (tile_rows, tile_cols) are distinct; slots from tile_counts[b, r, c] on are not part of the adjacency. `tile_counts`: some entry equals 12 in every draw.
All inputs are finite; a program needn't handle non-finite values.
Results may differ from the reference program's by a relative error of at most 0.02.
Values may be sent and summed in bfloat16 or wider, within the bound.
A program may use at most 64 MiB of HBM per device.

```python
import jax
import jax.numpy as jnp
from jax import lax

F = 256
TILE = 128
SLOTS = 12
ROWT = 2
NODES = 8192
N_BLK = 8
N_REP = 4


def tile_positions(key):
    places = N_REP * ROWT * ROWT
    scores = jax.random.randint(key, (N_BLK, N_REP, N_BLK, places), 0, 1 << 20) * places
    scores = scores + jnp.arange(places, dtype=jnp.int32)
    order = jnp.argsort(scores, axis=-1, stable=True)
    return order[..., :SLOTS].astype(jnp.int32)


def draw_tile_rows(key, part):
    chosen = tile_positions(key)
    return (chosen // ROWT).astype(jnp.int32)


def draw_tile_cols(key, part):
    chosen = tile_positions(key)
    return (chosen % ROWT).astype(jnp.int32)


def draw_tile_counts(key, part):
    key = jax.random.fold_in(key, 23)
    first, second, third = jax.random.split(key, 3)
    level = jax.random.randint(first, (N_BLK, 1, 1), (SLOTS + 2) // 3, SLOTS + 1)
    raw = jax.random.randint(second, (N_BLK, N_REP, N_BLK), 1, SLOTS + 1)
    counts = jnp.maximum(1, raw * level // SLOTS)
    spot = jax.random.randint(third, (), 0, N_BLK * N_REP * N_BLK)
    flat = jnp.arange(N_BLK * N_REP * N_BLK, dtype=jnp.int32).reshape(N_BLK, N_REP, N_BLK)
    return jnp.where(flat == spot, SLOTS, counts).astype(jnp.int32)


def draw_tile_values(key, part):
    key = jax.random.fold_in(key, 37)
    first, second = jax.random.split(key)
    shape = (N_BLK, N_REP, N_BLK, SLOTS, TILE, TILE)
    spread = (N_BLK * SLOTS * TILE / (24.0 * ROWT)) ** (-0.5)
    keep = jax.random.randint(second, shape, 0, 16) == 0
    values = jnp.clip(jax.random.normal(first, shape, jnp.float32), -6.0, 6.0)
    return jnp.where(keep, values * spread, 0.0).astype(jnp.bfloat16)


def block_scale(stream_key, extent, shards, least, top_value):
    gain = 1.0
    for axis_at, blocks in shards:
        draws = jax.random.uniform(jax.random.fold_in(jax.random.fold_in(stream_key, 6), axis_at), (blocks,), jnp.float32, least / len(shards), top_value / len(shards))
        gain = gain * jnp.repeat(jnp.exp(draws), extent[axis_at] // blocks).reshape((-1,) + (1,) * (len(extent) - 1 - axis_at))
    return gain


def noise(stream_key, dims, scale, reach, pieces=(), held_as=jnp.bfloat16):
    entries = scale * jax.random.normal(stream_key, dims, jnp.float32)
    if pieces:
        entries = entries * block_scale(stream_key, dims, pieces, -0.22, 0.18)
    return jnp.clip(entries, -reach, reach).astype(held_as)


def setup_inputs(seed: int = 0) -> dict:
    key_list = jax.random.split(jax.random.key(seed), 10)
    features = noise(key_list[0], (NODES, F), 1.0, 6.0, ((0, 32),))
    w_self = noise(key_list[1], (F, F), F ** -0.5, 0.375)
    w_neigh = noise(key_list[2], (F, F), F ** -0.5, 0.375)
    bias = noise(key_list[3], (F,), 0.5, 3.0, (), jnp.float32)
    cotangent = noise(key_list[4], (NODES, F), 1.0, 6.0, ((0, 32),))
    tile_values = draw_tile_values(jax.random.fold_in(key_list[9], 71), 0)
    tile_rows = draw_tile_rows(jax.random.fold_in(key_list[9], 71), 0)
    tile_cols = draw_tile_cols(jax.random.fold_in(key_list[9], 71), 0)
    tile_counts = draw_tile_counts(jax.random.fold_in(key_list[9], 71), 0)
    return {"features": features, "w_self": w_self, "w_neigh": w_neigh, "bias": bias, "cotangent": cotangent, "tile_values": tile_values, "tile_rows": tile_rows, "tile_cols": tile_cols, "tile_counts": tile_counts}


def reference(features, w_self, w_neigh, bias, cotangent, tile_values, tile_rows, tile_cols, tile_counts):
    blocks = features.reshape(N_BLK, N_REP, ROWT, TILE, F)
    column_ids = jnp.arange(N_BLK, dtype=jnp.int32)[:, None]
    slot_ids = jnp.arange(SLOTS, dtype=jnp.int32)[None, :]

    def partial_of(bidx, ridx):
        alive = slot_ids < tile_counts[bidx, ridx][:, None]
        gathered = blocks[column_ids, ridx, tile_cols[bidx, ridx]]
        prod = jnp.einsum('csij,csjf->csif', tile_values[bidx, ridx].astype(jnp.float32), gathered.astype(jnp.float32))
        prod = jnp.where(alive[:, :, None, None], prod, 0.0)
        total = jnp.zeros((N_REP * ROWT, TILE, F), jnp.float32)
        return total.at[tile_rows[bidx, ridx].reshape(-1)].add(prod.reshape(N_BLK * SLOTS, TILE, F))

    def agg_block(bidx):
        def per_slice(total, ridx):
            part = lax.optimization_barrier(partial_of(bidx, ridx).astype(jnp.bfloat16))
            return total + part.astype(jnp.float32), None
        total, unused = lax.scan(per_slice, jnp.zeros((N_REP * ROWT, TILE, F), jnp.float32), jnp.arange(N_REP, dtype=jnp.int32))
        return total

    agg = lax.map(agg_block, jnp.arange(N_BLK, dtype=jnp.int32)).reshape(NODES, F).astype(jnp.bfloat16)
    zvals = jnp.dot(features, w_self, preferred_element_type=jnp.float32) + jnp.dot(agg, w_neigh, preferred_element_type=jnp.float32) + bias
    sig = jax.nn.sigmoid(zvals)
    output = (zvals * sig).astype(jnp.bfloat16)
    dz = (cotangent.astype(jnp.float32) * sig * (1.0 + zvals * (1.0 - sig))).astype(jnp.bfloat16)
    grad_self = jnp.dot(features.T, dz, preferred_element_type=jnp.float32)
    grad_neigh = jnp.dot(agg.T, dz, preferred_element_type=jnp.float32)
    grad_bias = jnp.sum(dz.astype(jnp.float32), axis=0)
    dagg = jnp.dot(dz, w_neigh.T, preferred_element_type=jnp.float32).astype(jnp.bfloat16)
    dagg_blocks = dagg.reshape(N_BLK, N_REP * ROWT, TILE, F)

    def back_step(total, index):
        bidx = index // N_REP
        ridx = index % N_REP
        alive = slot_ids < tile_counts[bidx, ridx][:, None]
        picked = dagg_blocks[bidx][tile_rows[bidx, ridx]]
        term = jnp.einsum('csji,csjf->csif', tile_values[bidx, ridx].astype(jnp.float32), picked.astype(jnp.float32))
        term = jnp.where(alive[:, :, None, None], term, 0.0)
        placed = jnp.zeros((N_BLK, ROWT, TILE, F), jnp.float32).at[column_ids, tile_cols[bidx, ridx]].add(term)
        placed = lax.optimization_barrier(placed.astype(jnp.bfloat16)).astype(jnp.float32)
        return total.at[:, ridx].add(placed), None

    spread, unused = lax.scan(back_step, jnp.zeros((N_BLK, N_REP, ROWT, TILE, F), jnp.float32), jnp.arange(N_BLK * N_REP, dtype=jnp.int32))
    own = jnp.dot(dz, w_self.T, preferred_element_type=jnp.float32)
    grad_features = (own + spread.reshape(NODES, F)).astype(jnp.bfloat16)
    return output, grad_features, grad_self, grad_neigh, grad_bias
```

```python
import functools

import jax
import jax.numpy as jnp
from jax import lax
from jax.experimental import pallas as pl
from jax.experimental.pallas import tpu as pltpu
from jax.sharding import PartitionSpec as P

MESH = pl.DeviceIdType.MESH
F32 = jnp.float32
BF16 = jnp.bfloat16
PAD = 16


def dot_nn(a, b):
    return jnp.dot(a, b, preferred_element_type=F32)


def dot_nt(a, b):
    return lax.dot_general(a, b, (((1,), (1,)), ((), ())), preferred_element_type=F32)


def dot_tn(a, b):
    return lax.dot_general(a, b, (((0,), (0,)), ((), ())), preferred_element_type=F32)


def kernel(
    cfg,
    place_ref,
    x_ref,
    ws_ref,
    wn_ref,
    bias_ref,
    cot_ref,
    values_ref,
    out_ref,
    gradf_ref,
    gs_ref,
    gn_ref,
    gb_ref,
    vals,
    dense,
    xg,
    acc,
    zself,
    zsend,
    s1_recv,
    ysend,
    s2_recv,
    dg,
    yrecv,
    zrecv,
    gown,
    ga_send,
    ga_recv,
    gb_buf,
    gb_send,
    gc_buf,
    gc_send,
    gd_buf,
    ge_buf,
    vals_sem,
    x_rsem,
    x_ssem,
    s1_sems,
    s2_sems,
    dg_rsem,
    dg_ssem,
    y_sems,
    z_ssem,
    z_rsem,
    ga_sems,
    gb_sems,
    gc_sems,
    gd_sems,
    ge_sems,
    gf_sems,
):
    nblk, nrep, slots, tile, rows, width, scatter = cfg
    nz, chips = nblk // 2, nrep // 2
    per_dev = rows // tile
    rtiles = nrep * per_dev
    blk = lax.axis_index("blk")
    rep = lax.axis_index("rep")
    z, y = blk // 2, lax.rem(blk, 2)
    chip, core = rep // 2, lax.rem(rep, 2)
    oy, oc = 1 - y, 1 - core

    pending = []

    def send(src, dst, ssem, rsem, to_blk, to_rep, cond=None):
        copy = pltpu.make_async_remote_copy(
            src_ref=src,
            dst_ref=dst,
            send_sem=ssem,
            recv_sem=rsem,
            device_id=(to_blk, to_rep),
            device_id_type=MESH,
        )
        if cond is None:
            copy.start()
        else:
            pl.when(cond)(copy.start)
        pending.append((cond, copy))

    def arrived(dst, ssem, rsem):
        pltpu.make_async_remote_copy(
            src_ref=dst,
            dst_ref=dst,
            send_sem=ssem,
            recv_sem=rsem,
            device_id=(blk, rep),
            device_id_type=MESH,
        ).wait_recv()

    load = pltpu.make_async_copy(values_ref, vals.at[pl.ds(0, nblk * slots)], vals_sem)
    load.start()

    barrier = pltpu.get_barrier_semaphore()
    for i in range(1, nblk):
        pl.semaphore_signal(
            barrier, inc=1, device_id=(lax.rem(blk + i, nblk), rep), device_id_type=MESH
        )
    for i in range(1, nrep):
        pl.semaphore_signal(
            barrier, inc=1, device_id=(blk, lax.rem(rep + i, nrep)), device_id_type=MESH
        )
    pl.semaphore_wait(barrier, nblk + nrep - 2)

    def pass_on(src, origin, step, up, down):
        if up is not None:
            send(src, xg.at[origin], x_ssem.at[3 * step], x_rsem.at[origin], blk + 2, rep, up)
        if down is not None:
            send(src, xg.at[origin], x_ssem.at[3 * step + 1], x_rsem.at[origin], blk - 2, rep, down)

    def across(src, origin, sem_at, cond=None):
        send(src, xg.at[origin], x_ssem.at[sem_at], x_rsem.at[origin], z * 2 + oy, rep, cond)

    pass_on(x_ref, blk, 0, z < nz - 1, z > 0)
    across(x_ref, blk, 2)
    xg[blk] = x_ref[...]

    zself[...] = dot_nn(x_ref[...], ws_ref[...]) + bias_ref[...]
    vals[nblk * slots] = jnp.zeros((tile, tile), BF16)
    load.wait()

    def place_tiles(c, carry):
        def place_row(r):
            for t in range(per_dev):
                dense[c, pl.ds(r * tile, tile), t * tile : (t + 1) * tile] = vals[
                    place_ref[c, r * per_dev + t]
                ]

        if rtiles <= 8:
            for r in range(rtiles):
                place_row(r)
        else:
            pl.loop(0, rtiles)(place_row)
        return carry

    lax.fori_loop(0, nblk, place_tiles, 0)

    chunk = nrep * rows if nrep <= 4 else rows

    def add_block(c, first=False):
        def part(i):
            at = pl.ds(i * chunk, chunk)
            prod = dot_nn(dense[c, at, :], xg[c])
            if first:
                acc[at, :] = prod
            else:
                acc[at, :] += prod

        count = nrep * rows // chunk
        if count == 1:
            part(0)
        else:
            pl.loop(0, count)(part)

    add_block(blk, True)

    sem_base = 3 * nz
    for t in range(1, nz + 1):
        low, high = z - t, z + t
        if t < nz:
            olow, ohigh = low * 2 + y, high * 2 + y

            @pl.when(low >= 0)
            def _():
                arrived(xg.at[olow], x_ssem.at[0], x_rsem.at[olow])

            pass_on(xg.at[olow], olow, t, jnp.logical_and(low >= 0, z < nz - 1), None)
            across(xg.at[olow], olow, sem_base + 2 * t, low >= 0)

            @pl.when(high < nz)
            def _():
                arrived(xg.at[ohigh], x_ssem.at[0], x_rsem.at[ohigh])

            pass_on(xg.at[ohigh], ohigh, t, None, jnp.logical_and(high < nz, z > 0))
            across(xg.at[ohigh], ohigh, sem_base + 2 * t + 1, high < nz)

            @pl.when(low >= 0)
            def _():
                add_block(olow)

            @pl.when(high < nz)
            def _():
                add_block(ohigh)

        if t == 1:
            other = z * 2 + oy
            arrived(xg.at[other], x_ssem.at[0], x_rsem.at[other])
            add_block(other)
        else:
            plow, phigh = (z - (t - 1)) * 2 + oy, (z + (t - 1)) * 2 + oy

            @pl.when(z - (t - 1) >= 0)
            def _():
                arrived(xg.at[plow], x_ssem.at[0], x_rsem.at[plow])
                add_block(plow)

            @pl.when(z + (t - 1) < nz)
            def _():
                arrived(xg.at[phigh], x_ssem.at[0], x_rsem.at[phigh])
                add_block(phigh)

    mate = chip * 2 + oc
    before = len(pending)
    for i in range(chips):
        to = lax.rem(chip + 1 + i, chips)
        zsend[to] = acc[pl.ds((to * 2 + oc) * rows, rows), :].astype(BF16)
        send(zsend.at[to], s1_recv.at[to], s1_sems.at[0, to], s1_sems.at[1, to], blk, mate)
    total = None
    for i in range(chips):
        to = lax.rem(chip + 1 + i, chips)
        arrived(s1_recv.at[to], s1_sems.at[0, 0], s1_sems.at[1, to])
        part = acc[pl.ds((to * 2 + core) * rows, rows), :] + s1_recv[to].astype(F32)
        if i < chips - 1:
            ysend[to] = part.astype(BF16)
            send(
                ysend.at[to],
                s2_recv.at[chip],
                s2_sems.at[0, to],
                s2_sems.at[1, chip],
                blk,
                to * 2 + core,
            )
        else:
            total = part
    for i in range(chips - 1):
        frm = lax.rem(chip + 1 + i, chips)
        arrived(s2_recv.at[frm], s2_sems.at[0, 0], s2_sems.at[1, frm])
        total = total + s2_recv[frm].astype(F32)
    agg = total.astype(BF16)
    rep_sends = len(pending)

    zvals = zself[...] + dot_nn(agg, wn_ref[...])
    sig = jax.nn.sigmoid(zvals)
    out_ref[...] = (zvals * sig).astype(BF16)
    dz = (cot_ref[...].astype(F32) * sig * (1.0 + zvals * (1.0 - sig))).astype(BF16)
    dg[rep] = dot_nt(wn_ref[...], dz).astype(BF16)

    for i in range(chips - 1):
        to = lax.rem(chip + 1 + i, chips) * 2 + core
        send(dg.at[rep], dg.at[rep], dg_ssem.at[i], dg_rsem.at[rep], blk, to)
    send(dg.at[rep], dg.at[rep], dg_ssem.at[chips], dg_rsem.at[rep], blk, mate)

    gown[0] = dot_tn(x_ref[...], dz)
    gown[1] = dot_tn(agg, dz)
    gbias = jnp.broadcast_to(jnp.sum(dz.astype(F32), axis=0, keepdims=True), (PAD, width))
    ga_send[0:width, :] = gown[oc].astype(BF16)
    ga_send[width : width + PAD, :] = gbias.astype(BF16)
    send(ga_send, ga_recv, ga_sems.at[0], ga_sems.at[1], blk, mate)
    own = dot_nt(dz, ws_ref[...])

    for i in range(chips - 1):
        frm = lax.rem(chip + 1 + i, chips) * 2 + core
        arrived(dg.at[frm], dg_ssem.at[0], dg_rsem.at[frm])
        send(dg.at[frm], dg.at[frm], dg_ssem.at[chips + 1 + i], dg_rsem.at[frm], blk, mate)
    for i in range(chips):
        frm = lax.rem(chip + i, chips) * 2 + oc
        arrived(dg.at[frm], dg_ssem.at[0], dg_rsem.at[frm])

    for _, copy in pending[before:rep_sends]:
        copy.wait_send()
    del pending[before:rep_sends]

    def term(c):
        if nrep <= 4:
            out = dot_nn(dg[0], dense[c, 0:rows, :])
            for q in range(1, nrep):
                out = out + dot_nn(dg[q], dense[c, q * rows : (q + 1) * rows, :])
            return out

        def step(q, out):
            return out + dot_nn(dg[q], dense[c, pl.ds(q * rows, rows), :])

        return lax.fori_loop(0, nrep, step, jnp.zeros((width, rows), F32))

    def y_copy(dest):
        return pltpu.make_async_remote_copy(
            src_ref=ysend.at[dest],
            dst_ref=yrecv.at[dest],
            send_sem=y_sems.at[0, dest],
            recv_sem=y_sems.at[1, dest],
            device_id=(z * 2 + oy, rep),
            device_id_type=MESH,
        )

    turn = jnp.where(z < nz // 2, nz - 1, 1)

    def send_y(i, carry):
        dest = lax.rem(z + turn * (i + 1), nz)
        ysend[dest] = term(dest * 2 + oy).astype(BF16)
        y_copy(dest).start()
        return carry

    lax.fori_loop(0, nz, send_y, 0)

    def own_term(i, carry):
        acc[pl.ds(i * width, width), :] = term(i * 2 + y)
        return carry

    lax.fori_loop(0, nz, own_term, 0)

    arrived(ga_recv, ga_sems.at[0], ga_sems.at[1])
    share = width // scatter
    mine = gown[core] + ga_recv[0:width, :].astype(F32)
    gbias = gbias.astype(BF16).astype(F32) + ga_recv[width : width + PAD, :].astype(F32)
    gown[0] = mine
    if scatter == 1:
        gb_buf[chip, 0:share, :] = mine.astype(BF16)
    else:
        gb_buf[chip, 0:share, :] = gown[0, pl.ds(chip * share, share), :].astype(BF16)
    gb_buf[chip, share : share + PAD, :] = gbias.astype(BF16)
    for i in range(chips - 1):
        to = lax.rem(chip + 1 + i, chips)
        if scatter == 1:
            gb_send[i, 0:share, :] = mine.astype(BF16)
        else:
            gb_send[i, 0:share, :] = gown[0, pl.ds(to * share, share), :].astype(BF16)
        gb_send[i, share : share + PAD, :] = gbias.astype(BF16)
        send(
            gb_send.at[i],
            gb_buf.at[chip],
            gb_sems.at[0, i],
            gb_sems.at[1, chip],
            blk,
            to * 2 + core,
        )

    piece = share // nblk

    def grad_chips():
        for i in range(chips - 1):
            frm = lax.rem(chip + 1 + i, chips)
            arrived(gb_buf.at[frm], gb_sems.at[0, 0], gb_sems.at[1, frm])
        tot = gb_buf[0].astype(F32)
        for i in range(1, chips):
            tot = tot + gb_buf[i].astype(F32)
        for b in range(nblk):
            gc_send[b, 0:piece, :] = tot[b * piece : (b + 1) * piece].astype(BF16)
            gc_send[b, piece : piece + PAD, :] = tot[share : share + PAD].astype(BF16)
        gc_buf[blk] = gc_send[blk]
        for i in range(1, nblk):
            to = lax.rem(blk + i, nblk)
            send(gc_send.at[to], gc_buf.at[blk], gc_sems.at[0, to], gc_sems.at[1, blk], to, rep)

    def grad_blocks():
        for i in range(1, nblk):
            frm = lax.rem(blk + i, nblk)
            arrived(gc_buf.at[frm], gc_sems.at[0, 0], gc_sems.at[1, frm])
        tot = gc_buf[0].astype(F32)
        for b in range(1, nblk):
            tot = tot + gc_buf[b].astype(F32)
        gb_ref[...] = tot[piece : piece + 1]
        gd_buf[blk] = tot[0:piece].astype(BF16)
        for i in range(1, nblk):
            to = lax.rem(blk + i, nblk)
            send(gd_buf.at[blk], gd_buf.at[blk], gd_sems.at[0, to], gd_sems.at[1, blk], to, rep)

    def grad_back_blocks():
        for i in range(1, nblk):
            frm = lax.rem(blk + i, nblk)
            arrived(gd_buf.at[frm], gd_sems.at[0, 0], gd_sems.at[1, frm])
        for b in range(nblk):
            ge_buf[core, pl.ds(chip_at * share + b * piece, piece), :] = gd_buf[b]
        here = ge_buf.at[core, pl.ds(chip_at * share, share)]
        if scatter > 1:
            for i in range(chips - 1):
                to = lax.rem(chip + 1 + i, chips) * 2 + core
                send(here, here, ge_sems.at[0, i], ge_sems.at[1, chip], blk, to)

    def grad_back_chips():
        if scatter > 1:
            for i in range(chips - 1):
                frm = lax.rem(chip + 1 + i, chips)
                there = ge_buf.at[core, pl.ds(frm * share, share)]
                arrived(there, ge_sems.at[0, 0], ge_sems.at[1, frm])
        send(ge_buf.at[core], ge_buf.at[core], gf_sems.at[0], gf_sems.at[1], blk, mate)

    chip_at = chip if scatter > 1 else 0
    stages = [grad_chips, grad_blocks, grad_back_blocks, grad_back_chips]

    def gather_term(dest, src_dir, has_more):
        arrived(yrecv.at[dest], y_sems.at[0, 0], y_sems.at[1, dest])
        acc[pl.ds(dest * width, width), :] += yrecv[dest].astype(F32)

        @pl.when(has_more)
        def _():
            arrived(zrecv.at[src_dir, dest], z_ssem.at[0], z_rsem.at[src_dir, dest])
            acc[pl.ds(dest * width, width), :] += zrecv[src_dir, dest].astype(F32)

        zsend[dest] = acc[pl.ds(dest * width, width), :].astype(BF16)

    def chain_up(k, cond):
        dest = nz - 1 - k
        cond = jnp.logical_and(cond, z < dest)

        @pl.when(cond)
        def _():
            gather_term(dest, 0, z > 0)

        send(
            zsend.at[dest],
            zrecv.at[0, dest],
            z_ssem.at[dest],
            z_rsem.at[0, dest],
            blk + 2,
            rep,
            cond,
        )

    def chain_down(k):
        dest = k
        cond = z > dest

        @pl.when(cond)
        def _():
            gather_term(dest, 1, z < nz - 1)

        send(
            zsend.at[dest],
            zrecv.at[1, dest],
            z_ssem.at[dest],
            z_rsem.at[1, dest],
            blk - 2,
            rep,
            cond,
        )

    for k in range(nz - 1):
        chain_up(k, z < nz // 2)
        chain_down(k)
        chain_up(k, z >= nz // 2)
        if stages:
            stages.pop(0)()

    arrived(yrecv.at[z], y_sems.at[0, 0], y_sems.at[1, z])
    acc[pl.ds(z * width, width), :] += yrecv[z].astype(F32)

    @pl.when(z > 0)
    def _():
        arrived(zrecv.at[0, z], z_ssem.at[0], z_rsem.at[0, z])
        acc[pl.ds(z * width, width), :] += zrecv[0, z].astype(F32)

    @pl.when(z < nz - 1)
    def _():
        arrived(zrecv.at[1, z], z_ssem.at[0], z_rsem.at[1, z])
        acc[pl.ds(z * width, width), :] += zrecv[1, z].astype(F32)

    while stages:
        stages.pop(0)()

    gradf_ref[...] = (own + acc[pl.ds(z * width, width), :].T).astype(BF16)

    arrived(ge_buf.at[oc], gf_sems.at[0], gf_sems.at[1])
    gs_ref[...] = ge_buf[0].astype(F32)
    gn_ref[...] = ge_buf[1].astype(F32)

    for cond, copy in pending:
        if cond is None:
            copy.wait_send()
        else:
            pl.when(cond)(copy.wait_send)

    def drain_y(i, carry):
        y_copy(i).wait_send()
        return carry

    lax.fori_loop(0, nz, drain_y, 0)


def local(
    features, w_self, w_neigh, bias, cotangent, tile_values, tile_rows, tile_cols, tile_counts
):
    rows, width = features.shape
    nblk, nrep = lax.axis_size("blk"), lax.axis_size("rep")
    slots, tile = tile_values.shape[3], tile_values.shape[4]
    per_dev = rows // tile
    places = nrep * per_dev * per_dev
    nz, chips = nblk // 2, nrep // 2
    scatter = chips if width % (chips * nblk * 16) == 0 else 1
    share = width // scatter
    piece = share // nblk

    slot_place = tile_rows[0, 0] * per_dev + tile_cols[0, 0]
    slot_ids = lax.broadcasted_iota(jnp.int32, (nblk, slots), 1)
    slot_place = jnp.where(slot_ids < tile_counts[0, 0][:, None], slot_place, -1)
    flat = lax.broadcasted_iota(jnp.int32, (nblk, slots), 0) * slots + slot_ids
    empty = nblk * slots
    hit = slot_place[:, :, None] == lax.broadcasted_iota(jnp.int32, (1, 1, places), 2)
    place = empty + jnp.sum(jnp.where(hit, flat[:, :, None] - empty, 0), axis=1)

    cfg = (nblk, nrep, slots, tile, rows, width, scatter)
    vmem = pl.BlockSpec(memory_space=pltpu.VMEM)
    sems = pltpu.SemaphoreType.DMA
    outs = pl.pallas_call(
        functools.partial(kernel, cfg),
        out_shape=(
            jax.ShapeDtypeStruct((rows, width), BF16),
            jax.ShapeDtypeStruct((rows, width), BF16),
            jax.ShapeDtypeStruct((width, width), F32),
            jax.ShapeDtypeStruct((width, width), F32),
            jax.ShapeDtypeStruct((1, width), F32),
        ),
        in_specs=[
            pl.BlockSpec(memory_space=pltpu.SMEM),
            vmem,
            vmem,
            vmem,
            vmem,
            vmem,
            pl.BlockSpec(memory_space=pl.ANY),
        ],
        out_specs=(vmem,) * 5,
        scratch_shapes=[
            pltpu.VMEM((nblk * slots + 1, tile, tile), BF16),
            pltpu.VMEM((nblk, nrep * rows, rows), BF16),
            pltpu.VMEM((nblk, rows, width), BF16),
            pltpu.VMEM((max(nrep * rows, nz * width), width), F32),
            pltpu.VMEM((rows, width), F32),
            pltpu.VMEM((max(chips, nz), rows, width), BF16),
            pltpu.VMEM((chips, rows, width), BF16),
            pltpu.VMEM((max(chips, nz), rows, width), BF16),
            pltpu.VMEM((chips, rows, width), BF16),
            pltpu.VMEM((nrep, width, rows), BF16),
                pltpu.VMEM((nz, width, rows), BF16),
            pltpu.VMEM((2, nz, width, rows), BF16),
            pltpu.VMEM((2, width, width), F32),
            pltpu.VMEM((width + PAD, width), BF16),
            pltpu.VMEM((width + PAD, width), BF16),
            pltpu.VMEM((chips, share + PAD, width), BF16),
            pltpu.VMEM((chips, share + PAD, width), BF16),
            pltpu.VMEM((nblk, piece + PAD, width), BF16),
            pltpu.VMEM((nblk, piece + PAD, width), BF16),
            pltpu.VMEM((nblk, piece, width), BF16),
            pltpu.VMEM((2, width, width), BF16),
            sems,
            sems((nblk,)),
            sems((5 * nz,)),
            sems((2, chips)),
            sems((2, chips)),
            sems((nrep,)),
            sems((2 * chips + 1,)),
            sems((2, nz)),
            sems((nz,)),
            sems((2, nz)),
            sems((2,)),
            sems((2, chips)),
            sems((2, nblk)),
            sems((2, nblk)),
            sems((2, chips)),
            sems((2,)),
        ],
        compiler_params=pltpu.CompilerParams(
            collective_id=0, has_side_effects=True, vmem_limit_bytes=60 * 1024 * 1024
        ),
        cost_estimate=pl.CostEstimate(
            flops=4 * nblk * nrep * rows * rows * width,
            bytes_accessed=nblk * slots * tile * tile * 2,
            transcendentals=rows * width,
        ),
    )(
        place,
        features,
        w_self,
        w_neigh,
        bias.reshape(1, width),
        cotangent,
        tile_values.reshape(nblk * slots, tile, tile),
    )
    output, grad_features, grad_self, grad_neigh, grad_bias = outs
    return output, grad_features, grad_self, grad_neigh, grad_bias.reshape(width)


def solution(mesh):
    in_specs = (
        P(("blk", "rep"), None),
        P(),
        P(),
        P(),
        P(("blk", "rep"), None),
        P("blk", "rep", None, None, None, None),
        P("blk", "rep", None, None),
        P("blk", "rep", None, None),
        P("blk", "rep", None),
    )
    out_specs = (P(("blk", "rep"), None), P(("blk", "rep"), None), P(), P(), P())
    return jax.shard_map(local, mesh=mesh, in_specs=in_specs, out_specs=out_specs, check_vma=False)
```

```python
import functools

import jax
import jax.numpy as jnp
from jax import lax
from jax.experimental import pallas as pl
from jax.experimental.pallas import tpu as pltpu
from jax.sharding import PartitionSpec as P

MESH = pl.DeviceIdType.MESH
F32 = jnp.float32
BF16 = jnp.bfloat16
PAD = 16


def dot_nn(a, b):
    return jnp.dot(a, b, preferred_element_type=F32)


def dot_nt(a, b):
    return lax.dot_general(a, b, (((1,), (1,)), ((), ())), preferred_element_type=F32)


def dot_tn(a, b):
    return lax.dot_general(a, b, (((0,), (0,)), ((), ())), preferred_element_type=F32)


def kernel(
    cfg,
    place_ref,
    x_ref,
    ws_ref,
    wn_ref,
    bias_ref,
    cot_ref,
    values_ref,
    out_ref,
    gradf_ref,
    ge_ref,
    gb_ref,
    vals,
    dense,
    xg,
    acc,
    zself,
    zsend,
    s1_recv,
    ysend,
    s2_recv,
    dg,
    yrecv,
    zrecv,
    gown,
    ga_send,
    ga_recv,
    gb_buf,
    gc_buf,
    gc_send,
    ge_buf,
    vals_sem,
    x_rsem,
    x_ssem,
    s1_sems,
    s2_sems,
    dg_rsem,
    dg_ssem,
    y_sems,
    z_ssem,
    z_rsem,
    ga_sems,
    gb_sems,
    gc_sems,
    gd_sems,
    gf_sems,
):
    nblk, nrep, slots, tile, rows, width = cfg
    nz, chips = nblk // 2, nrep // 2
    per_dev = rows // tile
    rtiles = nrep * per_dev
    blk = lax.axis_index("blk")
    rep = lax.axis_index("rep")
    z, y = blk // 2, lax.rem(blk, 2)
    chip, core = rep // 2, lax.rem(rep, 2)
    oy, oc = 1 - y, 1 - core

    pending = []

    def send(src, dst, ssem, rsem, to_blk, to_rep, cond=None):
        copy = pltpu.make_async_remote_copy(
            src_ref=src,
            dst_ref=dst,
            send_sem=ssem,
            recv_sem=rsem,
            device_id=(to_blk, to_rep),
            device_id_type=MESH,
        )
        if cond is None:
            copy.start()
        else:
            pl.when(cond)(copy.start)
        pending.append((cond, copy))

    def arrived(dst, ssem, rsem):
        pltpu.make_async_remote_copy(
            src_ref=dst,
            dst_ref=dst,
            send_sem=ssem,
            recv_sem=rsem,
            device_id=(blk, rep),
            device_id_type=MESH,
        ).wait_recv()

    load = pltpu.make_async_copy(values_ref, vals.at[pl.ds(0, nblk * slots)], vals_sem)
    load.start()

    barrier = pltpu.get_barrier_semaphore()
    for i in range(1, nblk):
        pl.semaphore_signal(
            barrier, inc=1, device_id=(lax.rem(blk + i, nblk), rep), device_id_type=MESH
        )
    for i in range(1, nrep):
        pl.semaphore_signal(
            barrier, inc=1, device_id=(blk, lax.rem(rep + i, nrep)), device_id_type=MESH
        )
    pl.semaphore_wait(barrier, nblk + nrep - 2)

    half = rows // 2

    def pass_on(src, origin, step, h, kind, to_blk, cond):
        send(
            src.at[pl.ds(h * half, half)],
            xg.at[origin, pl.ds(h * half, half)],
            x_ssem.at[step, h, kind],
            x_rsem.at[origin, h],
            to_blk,
            rep,
            cond,
        )

    def half_arrived(origin, h):
        arrived(xg.at[origin, pl.ds(h * half, half)], x_ssem.at[0, 0, 0], x_rsem.at[origin, h])

    for h in range(2):
        pass_on(x_ref, blk, 0, h, 0, blk + 2, z < nz - 1)
        pass_on(x_ref, blk, 0, h, 1, blk - 2, z > 0)
        pass_on(x_ref, blk, 0, h, 2, z * 2 + oy, None)
    xg[blk] = x_ref[...]

    zself[...] = dot_nn(x_ref[...], ws_ref[...]) + bias_ref[...]
    vals[nblk * slots] = jnp.zeros((tile, tile), BF16)
    load.wait()

    def place_tiles(c, carry):
        def place_row(r):
            for t in range(per_dev):
                dense[c, pl.ds(r * tile, tile), t * tile : (t + 1) * tile] = vals[
                    place_ref[c, r * per_dev + t]
                ]

        if rtiles <= 8:
            for r in range(rtiles):
                place_row(r)
        else:
            pl.loop(0, rtiles)(place_row)
        return carry

    lax.fori_loop(0, nblk, place_tiles, 0)

    chunk = nrep * rows if nrep <= 4 else rows

    def add_block(c, first=False):
        def part(i):
            at = pl.ds(i * chunk, chunk)
            prod = dot_nn(dense[c, at, :], xg[c])
            if first:
                acc[at, :] = prod
            else:
                acc[at, :] += prod

        count = nrep * rows // chunk
        if count == 1:
            part(0)
        else:
            pl.loop(0, count)(part)

    add_block(blk, True)

    def add_pair(step, side, wait):
        for at in (z - step, z + step):
            origin = at * 2 + side

            @pl.when(jnp.logical_and(at >= 0, at < nz))
            def _():
                if wait:
                    half_arrived(origin, 0)
                    half_arrived(origin, 1)
                add_block(origin)

    for t in range(1, nz):
        for h in range(2):
            for at, kind, inner in ((z - t, 0, z < nz - 1), (z + t, 1, z > 0)):
                origin = at * 2 + y
                there = at >= 0 if kind == 0 else at < nz
                on = blk + 2 if kind == 0 else blk - 2

                @pl.when(there)
                def _():
                    half_arrived(origin, h)

                held = xg.at[origin]
                pass_on(held, origin, t, h, kind, on, jnp.logical_and(there, inner))
                pass_on(held, origin, t, h, kind + 2, z * 2 + oy, there)
        add_pair(t, y, False)
        if t == 1:
            half_arrived(z * 2 + oy, 0)
            half_arrived(z * 2 + oy, 1)
            add_block(z * 2 + oy)
        else:
            add_pair(t - 1, oy, True)
    add_pair(nz - 1, oy, True)

    mate = chip * 2 + oc
    before = len(pending)
    for i in range(chips):
        to = lax.rem(chip + 1 + i, chips)
        zsend[to] = acc[pl.ds((to * 2 + oc) * rows, rows), :].astype(BF16)
        send(zsend.at[to], s1_recv.at[to], s1_sems.at[0, to], s1_sems.at[1, to], blk, mate)
    total = None
    for i in range(chips):
        to = lax.rem(chip + 1 + i, chips)
        arrived(s1_recv.at[to], s1_sems.at[0, 0], s1_sems.at[1, to])
        part = acc[pl.ds((to * 2 + core) * rows, rows), :] + s1_recv[to].astype(F32)
        if i < chips - 1:
            ysend[to] = part.astype(BF16)
            send(
                ysend.at[to],
                s2_recv.at[chip],
                s2_sems.at[0, to],
                s2_sems.at[1, chip],
                blk,
                to * 2 + core,
            )
        else:
            total = part
    for i in range(chips - 1):
        frm = lax.rem(chip + 1 + i, chips)
        arrived(s2_recv.at[frm], s2_sems.at[0, 0], s2_sems.at[1, frm])
        total = total + s2_recv[frm].astype(F32)
    agg = total.astype(BF16)
    rep_sends = len(pending)

    zvals = zself[...] + dot_nn(agg, wn_ref[...])
    sig = jax.nn.sigmoid(zvals)
    out_ref[...] = (zvals * sig).astype(BF16)
    dz = (cot_ref[...].astype(F32) * sig * (1.0 + zvals * (1.0 - sig))).astype(BF16)
    dg[rep] = dot_nt(wn_ref[...], dz).astype(BF16)

    for i in range(chips - 1):
        to = lax.rem(chip + 1 + i, chips) * 2 + core
        send(dg.at[rep], dg.at[rep], dg_ssem.at[i], dg_rsem.at[rep], blk, to)
    send(dg.at[rep], dg.at[rep], dg_ssem.at[chips], dg_rsem.at[rep], blk, mate)

    gown[0] = dot_tn(x_ref[...], dz)
    gown[1] = dot_tn(agg, dz)
    gbias = jnp.broadcast_to(jnp.sum(dz.astype(F32), axis=0, keepdims=True), (PAD, width))
    ga_send[0:width, :] = gown[oc].astype(BF16)
    ga_send[width : width + PAD, :] = gbias.astype(BF16)
    send(ga_send, ga_recv, ga_sems.at[0], ga_sems.at[1], blk, mate)
    own = dot_nt(dz, ws_ref[...])
    piece = width // nblk

    arrived(ga_recv, ga_sems.at[0], ga_sems.at[1])
    gbias = gbias.astype(BF16).astype(F32) + ga_recv[width : width + PAD, :].astype(F32)
    gown[0] = gown[core] + ga_recv[0:width, :].astype(F32)
    for b in range(nblk):
        gc_send[b, 0:piece, :] = gown[0, b * piece : (b + 1) * piece].astype(BF16)
        gc_send[b, piece : piece + PAD, :] = gbias.astype(BF16)
    gc_buf[blk] = gc_send[blk]
    for i in range(1, nblk):
        to = lax.rem(blk + i, nblk)
        send(gc_send.at[to], gc_buf.at[blk], gc_sems.at[0, to], gc_sems.at[1, blk], to, rep)

    for i in range(chips - 1):
        frm = lax.rem(chip + 1 + i, chips) * 2 + core
        arrived(dg.at[frm], dg_ssem.at[0], dg_rsem.at[frm])
        send(dg.at[frm], dg.at[frm], dg_ssem.at[chips + 1 + i], dg_rsem.at[frm], blk, mate)
    for i in range(chips):
        frm = lax.rem(chip + i, chips) * 2 + oc
        arrived(dg.at[frm], dg_ssem.at[0], dg_rsem.at[frm])

    for _, copy in pending[before:rep_sends]:
        copy.wait_send()
    del pending[before:rep_sends]

    def term(c):
        if nrep <= 4:
            out = dot_nn(dg[0], dense[c, 0:rows, :])
            for q in range(1, nrep):
                out = out + dot_nn(dg[q], dense[c, q * rows : (q + 1) * rows, :])
            return out

        def step(q, out):
            return out + dot_nn(dg[q], dense[c, pl.ds(q * rows, rows), :])

        return lax.fori_loop(0, nrep, step, jnp.zeros((width, rows), F32))

    fhalf = width // 2

    def y_copy(dest, h):
        at = pl.ds(h * fhalf, fhalf)
        return pltpu.make_async_remote_copy(
            src_ref=ysend.at[dest, at],
            dst_ref=yrecv.at[dest, at],
            send_sem=y_sems.at[0, dest, h],
            recv_sem=y_sems.at[1, dest, h],
            device_id=(z * 2 + oy, rep),
            device_id_type=MESH,
        )

    near = jnp.minimum(z, nz - 1 - z)

    def send_y(i, carry):
        dest = jnp.where(
            i < 2 * near,
            jnp.where(lax.rem(i, 2) == 0, nz - 1 - i // 2, i // 2),
            nz - 1 - (i - near),
        )
        dest = jnp.where(z < nz // 2, dest, nz - 1 - dest)
        ysend[dest] = term(dest * 2 + oy).astype(BF16)
        y_copy(dest, 0).start()
        y_copy(dest, 1).start()
        return carry

    lax.fori_loop(0, nz, send_y, 0)

    def own_term(i, carry):
        acc[pl.ds(i * width, width), :] = term(i * 2 + y)
        return carry

    lax.fori_loop(0, nz, own_term, 0)

    def grad_sums():
        for i in range(1, nblk):
            frm = lax.rem(blk + i, nblk)
            arrived(gc_buf.at[frm], gc_sems.at[0, 0], gc_sems.at[1, frm])
        tot = gc_buf[0].astype(F32)
        for b in range(1, nblk):
            tot = tot + gc_buf[b].astype(F32)
        gb_buf[chip] = tot.astype(BF16)
        for i in range(chips - 1):
            to = lax.rem(chip + 1 + i, chips)
            send(
                gb_buf.at[chip],
                gb_buf.at[chip],
                gb_sems.at[0, i],
                gb_sems.at[1, chip],
                blk,
                to * 2 + core,
            )
        for i in range(chips - 1):
            frm = lax.rem(chip + 1 + i, chips)
            arrived(gb_buf.at[frm], gb_sems.at[0, 0], gb_sems.at[1, frm])
        tot = gb_buf[0].astype(F32)
        for i in range(1, chips):
            tot = tot + gb_buf[i].astype(F32)
        gb_ref[...] = tot[piece : piece + 1]
        here = ge_buf.at[core, pl.ds(blk * piece, piece)]
        ge_buf[core, pl.ds(blk * piece, piece), :] = tot[0:piece].astype(BF16)
        for i in range(1, nblk):
            to = lax.rem(blk + i, nblk)
            send(here, here, gd_sems.at[0, to], gd_sems.at[1, blk], to, rep)

    def grad_back():
        for i in range(1, nblk):
            frm = lax.rem(blk + i, nblk)
            arrived(
                ge_buf.at[core, pl.ds(frm * piece, piece)], gd_sems.at[0, 0], gd_sems.at[1, frm]
            )
        send(ge_buf.at[core], ge_buf.at[core], gf_sems.at[0], gf_sems.at[1], blk, mate)

    def add_from(buf, dest, h, sem):
        at = pl.ds(dest * width + h * fhalf, fhalf)
        arrived(buf.at[pl.ds(h * fhalf, fhalf)], z_ssem.at[0, 0], sem)
        acc[at, :] += buf[h * fhalf : (h + 1) * fhalf, :].astype(F32)

    def chain(k, way, cond):
        dest = nz - 1 - k if way == 0 else k
        on = blk + 2 if way == 0 else blk - 2
        more = z > 0 if way == 0 else z < nz - 1
        cond = jnp.logical_and(cond, z < dest if way == 0 else z > dest)
        for h in range(2):

            @pl.when(cond)
            def _():
                add_from(yrecv.at[dest], dest, h, y_sems.at[1, dest, h])

                @pl.when(more)
                def _():
                    add_from(zrecv.at[way, dest], dest, h, z_rsem.at[way, dest, h])

                rows_at = pl.ds(dest * width + h * fhalf, fhalf)
                zsend[dest, h * fhalf : (h + 1) * fhalf, :] = acc[rows_at, :].astype(BF16)

            at = pl.ds(h * fhalf, fhalf)
            send(
                zsend.at[dest, at],
                zrecv.at[way, dest, at],
                z_ssem.at[dest, h],
                z_rsem.at[way, dest, h],
                on,
                rep,
                cond,
            )

    at_end = near == 0
    chain(0, 0, z == 0)
    chain(0, 1, z == nz - 1)
    grad_sums()
    for k in range(nz - 1):
        inside = z >= 0 if k else jnp.logical_not(at_end)
        chain(k, 0, jnp.logical_and(inside, z < nz // 2))
        chain(k, 1, inside)
        chain(k, 0, jnp.logical_and(inside, z >= nz // 2))

    grad_back()
    for h in range(2):
        add_from(yrecv.at[z], z, h, y_sems.at[1, z, h])

        @pl.when(z > 0)
        def _():
            add_from(zrecv.at[0, z], z, h, z_rsem.at[0, z, h])

        @pl.when(z < nz - 1)
        def _():
            add_from(zrecv.at[1, z], z, h, z_rsem.at[1, z, h])

    gradf_ref[...] = (own + acc[pl.ds(z * width, width), :].T).astype(BF16)

    arrived(ge_buf.at[oc], gf_sems.at[0], gf_sems.at[1])
    ge_ref[...] = ge_buf[...]

    for cond, copy in pending:
        if cond is None:
            copy.wait_send()
        else:
            pl.when(cond)(copy.wait_send)

    def drain_y(i, carry):
        y_copy(i, 0).wait_send()
        y_copy(i, 1).wait_send()
        return carry

    lax.fori_loop(0, nz, drain_y, 0)


def hand_out(a_ref, b_ref, c_ref, d_ref, out_ref, gradf_ref, gs_ref, gn_ref, gb_ref):
    out_ref[...] = a_ref[...]
    gradf_ref[...] = b_ref[...]
    gs_ref[...] = c_ref[0].astype(F32)
    gn_ref[...] = c_ref[1].astype(F32)
    gb_ref[...] = d_ref[...]


def local(
    features, w_self, w_neigh, bias, cotangent, tile_values, tile_rows, tile_cols, tile_counts
):
    rows, width = features.shape
    nblk, nrep = lax.axis_size("blk"), lax.axis_size("rep")
    slots, tile = tile_values.shape[3], tile_values.shape[4]
    per_dev = rows // tile
    places = nrep * per_dev * per_dev
    nz, chips = nblk // 2, nrep // 2
    piece = width // nblk

    slot_place = tile_rows[0, 0] * per_dev + tile_cols[0, 0]
    slot_ids = lax.broadcasted_iota(jnp.int32, (nblk, slots), 1)
    slot_place = jnp.where(slot_ids < tile_counts[0, 0][:, None], slot_place, -1)
    flat = lax.broadcasted_iota(jnp.int32, (nblk, slots), 0) * slots + slot_ids
    empty = nblk * slots
    hit = slot_place[:, :, None] == lax.broadcasted_iota(jnp.int32, (1, 1, places), 2)
    place = empty + jnp.sum(jnp.where(hit, flat[:, :, None] - empty, 0), axis=1)

    cfg = (nblk, nrep, slots, tile, rows, width)
    vmem = pl.BlockSpec(memory_space=pltpu.VMEM)
    sems = pltpu.SemaphoreType.DMA
    outs = pl.pallas_call(
        functools.partial(kernel, cfg),
        out_shape=(
            jax.ShapeDtypeStruct((rows, width), BF16),
            jax.ShapeDtypeStruct((rows, width), BF16),
            jax.ShapeDtypeStruct((2, width, width), BF16),
            jax.ShapeDtypeStruct((1, width), F32),
        ),
        in_specs=[
            pl.BlockSpec(memory_space=pltpu.SMEM),
            vmem,
            vmem,
            vmem,
            vmem,
            vmem,
            pl.BlockSpec(memory_space=pl.ANY),
        ],
        out_specs=(vmem,) * 4,
        scratch_shapes=[
            pltpu.VMEM((nblk * slots + 1, tile, tile), BF16),
            pltpu.VMEM((nblk, nrep * rows, rows), BF16),
            pltpu.VMEM((nblk, rows, width), BF16),
            pltpu.VMEM((max(nrep * rows, nz * width), width), F32),
            pltpu.VMEM((rows, width), F32),
            pltpu.VMEM((max(chips, nz), rows, width), BF16),
            pltpu.VMEM((chips, rows, width), BF16),
            pltpu.VMEM((max(chips, nz), rows, width), BF16),
            pltpu.VMEM((chips, rows, width), BF16),
            pltpu.VMEM((nrep, width, rows), BF16),
                pltpu.VMEM((nz, width, rows), BF16),
            pltpu.VMEM((2, nz, width, rows), BF16),
            pltpu.VMEM((2, width, width), F32),
            pltpu.VMEM((width + PAD, width), BF16),
            pltpu.VMEM((width + PAD, width), BF16),
            pltpu.VMEM((chips, piece + PAD, width), BF16),
            pltpu.VMEM((nblk, piece + PAD, width), BF16),
            pltpu.VMEM((nblk, piece + PAD, width), BF16),
            pltpu.VMEM((2, width, width), BF16),
            sems,
            sems((nblk, 2)),
            sems((nz, 2, 4)),
            sems((2, chips)),
            sems((2, chips)),
            sems((nrep,)),
            sems((2 * chips + 1,)),
            sems((2, nz, 2)),
            sems((nz, 2)),
            sems((2, nz, 2)),
            sems((2,)),
            sems((2, chips)),
            sems((2, nblk)),
            sems((2, nblk)),
            sems((2,)),
        ],
        compiler_params=pltpu.CompilerParams(
            collective_id=0, has_side_effects=True, vmem_limit_bytes=60 * 1024 * 1024
        ),
        cost_estimate=pl.CostEstimate(
            flops=4 * nblk * nrep * rows * rows * width,
            bytes_accessed=nblk * slots * tile * tile * 2,
            transcendentals=rows * width,
        ),
    )(
        place,
        features,
        w_self,
        w_neigh,
        bias.reshape(1, width),
        cotangent,
        tile_values.reshape(nblk * slots, tile, tile),
    )
    output, grad_features, grad_self, grad_neigh, grad_bias = pl.pallas_call(
        hand_out,
        out_shape=(
            jax.ShapeDtypeStruct((rows, width), BF16),
            jax.ShapeDtypeStruct((rows, width), BF16),
            jax.ShapeDtypeStruct((width, width), F32),
            jax.ShapeDtypeStruct((width, width), F32),
            jax.ShapeDtypeStruct((1, width), F32),
        ),
        in_specs=[vmem] * 4,
        out_specs=(vmem,) * 5,
    )(*outs)
    return output, grad_features, grad_self, grad_neigh, grad_bias.reshape(width)


def solution(mesh):
    in_specs = (
        P(("blk", "rep"), None),
        P(),
        P(),
        P(),
        P(("blk", "rep"), None),
        P("blk", "rep", None, None, None, None),
        P("blk", "rep", None, None),
        P("blk", "rep", None, None),
        P("blk", "rep", None),
    )
    out_specs = (P(("blk", "rep"), None), P(("blk", "rep"), None), P(), P(), P())
    return jax.shard_map(local, mesh=mesh, in_specs=in_specs, out_specs=out_specs, check_vma=False)
```

```python
import functools

import jax
import jax.numpy as jnp
from jax import lax
from jax.experimental import pallas as pl
from jax.experimental.pallas import tpu as pltpu
from jax.sharding import PartitionSpec as P

MESH = pl.DeviceIdType.MESH
F32 = jnp.float32
BF16 = jnp.bfloat16
PAD = 16


def dot_nn(a, b):
    return jnp.dot(a, b, preferred_element_type=F32)


def dot_nt(a, b):
    return lax.dot_general(a, b, (((1,), (1,)), ((), ())), preferred_element_type=F32)


def dot_tn(a, b):
    return lax.dot_general(a, b, (((0,), (0,)), ((), ())), preferred_element_type=F32)


def kernel(
    cfg,
    counts_ref,
    trows_ref,
    tcols_ref,
    x_ref,
    ws_ref,
    wn_ref,
    bias_ref,
    cot_ref,
    values_ref,
    out_ref,
    gradf_ref,
    ge_ref,
    gb_ref,
    vals,
    dense,
    xg,
    acc,
    zself,
    zsend,
    s1_recv,
    ysend,
    s2_recv,
    dg,
    yrecv,
    zrecv,
    gown,
    ga_send,
    ga_recv,
    gb_buf,
    gc_buf,
    gc_send,
    ge_buf,
    place_vec,
    place_ref,
    vals_sem,
    place_sem,
    x_rsem,
    x_ssem,
    s1_sems,
    s2_sems,
    dg_rsem,
    dg_ssem,
    y_sems,
    z_ssem,
    z_rsem,
    ga_sems,
    gb_sems,
    gc_sems,
    gd_sems,
    gf_sems,
):
    nblk, nrep, slots, tile, rows, width = cfg
    nz, chips = nblk // 2, nrep // 2
    per_dev = rows // tile
    rtiles = nrep * per_dev
    blk = lax.axis_index("blk")
    rep = lax.axis_index("rep")
    z, y = blk // 2, lax.rem(blk, 2)
    chip, core = rep // 2, lax.rem(rep, 2)
    oy, oc = 1 - y, 1 - core

    pending = []

    def send(src, dst, ssem, rsem, to_blk, to_rep, cond=None):
        copy = pltpu.make_async_remote_copy(
            src_ref=src,
            dst_ref=dst,
            send_sem=ssem,
            recv_sem=rsem,
            device_id=(to_blk, to_rep),
            device_id_type=MESH,
        )
        if cond is None:
            copy.start()
        else:
            pl.when(cond)(copy.start)
        pending.append((cond, copy))

    def arrived(dst, ssem, rsem):
        pltpu.make_async_remote_copy(
            src_ref=dst,
            dst_ref=dst,
            send_sem=ssem,
            recv_sem=rsem,
            device_id=(blk, rep),
            device_id_type=MESH,
        ).wait_recv()

    load = pltpu.make_async_copy(values_ref, vals.at[pl.ds(0, nblk * slots)], vals_sem)
    load.start()

    lanes = place_vec.shape[1]
    row_at = lax.broadcasted_iota(jnp.int32, (nblk, lanes), 0)
    lane = lax.broadcasted_iota(jnp.int32, (nblk, lanes), 1)

    def find_places():
        live = jnp.zeros((nblk, lanes), jnp.int32)
        for c in range(nblk):
            live = jnp.where(row_at == c, counts_ref[0, c], live)
        at = trows_ref[...] * per_dev + tcols_ref[...]
        found = jnp.full((nblk, lanes), nblk * slots, jnp.int32)
        for slot in range(slots):
            hit = jnp.logical_and(at[:, slot : slot + 1] == lane, live > slot)
            found = jnp.where(hit, row_at * slots + slot, found)
        place_vec[...] = found
        move = pltpu.make_async_copy(place_vec, place_ref, place_sem)
        move.start()
        return move

    barrier = pltpu.get_barrier_semaphore()
    for i in range(1, nblk):
        pl.semaphore_signal(
            barrier, inc=1, device_id=(lax.rem(blk + i, nblk), rep), device_id_type=MESH
        )
    for i in range(1, nrep):
        pl.semaphore_signal(
            barrier, inc=1, device_id=(blk, lax.rem(rep + i, nrep)), device_id_type=MESH
        )
    pl.semaphore_wait(barrier, nblk + nrep - 2)

    half = rows // 2

    def pass_on(src, origin, step, h, kind, to_blk, cond):
        send(
            src.at[pl.ds(h * half, half)],
            xg.at[origin, pl.ds(h * half, half)],
            x_ssem.at[step, h, kind],
            x_rsem.at[origin, h],
            to_blk,
            rep,
            cond,
        )

    def half_arrived(origin, h):
        arrived(xg.at[origin, pl.ds(h * half, half)], x_ssem.at[0, 0, 0], x_rsem.at[origin, h])

    for h in range(2):
        pass_on(x_ref, blk, 0, h, 0, blk + 2, z < nz - 1)
        pass_on(x_ref, blk, 0, h, 1, blk - 2, z > 0)
        pass_on(x_ref, blk, 0, h, 2, z * 2 + oy, None)
    xg[blk] = x_ref[...]

    move = find_places()
    zself[...] = dot_nn(x_ref[...], ws_ref[...]) + bias_ref[...]
    vals[nblk * slots] = jnp.zeros((tile, tile), BF16)
    move.wait()
    load.wait()

    def place_tiles(c, carry):
        def place_row(r):
            for t in range(per_dev):
                dense[c, pl.ds(r * tile, tile), t * tile : (t + 1) * tile] = vals[
                    place_ref[c, r * per_dev + t]
                ]

        if rtiles <= 8:
            for r in range(rtiles):
                place_row(r)
        else:
            pl.loop(0, rtiles)(place_row)
        return carry

    lax.fori_loop(0, nblk, place_tiles, 0)

    chunk = nrep * rows if nrep <= 4 else rows

    def add_block(c, first=False):
        def part(i):
            at = pl.ds(i * chunk, chunk)
            prod = dot_nn(dense[c, at, :], xg[c])
            if first:
                acc[at, :] = prod
            else:
                acc[at, :] += prod

        count = nrep * rows // chunk
        if count == 1:
            part(0)
        else:
            pl.loop(0, count)(part)

    add_block(blk, True)

    def add_pair(step, side, wait):
        for at in (z - step, z + step):
            origin = at * 2 + side

            @pl.when(jnp.logical_and(at >= 0, at < nz))
            def _():
                if wait:
                    half_arrived(origin, 0)
                    half_arrived(origin, 1)
                add_block(origin)

    for t in range(1, nz):
        for h in range(2):
            for at, kind, inner in ((z - t, 0, z < nz - 1), (z + t, 1, z > 0)):
                origin = at * 2 + y
                there = at >= 0 if kind == 0 else at < nz
                on = blk + 2 if kind == 0 else blk - 2

                @pl.when(there)
                def _():
                    half_arrived(origin, h)

                held = xg.at[origin]
                pass_on(held, origin, t, h, kind, on, jnp.logical_and(there, inner))
                pass_on(held, origin, t, h, kind + 2, z * 2 + oy, there)
        add_pair(t, y, False)
        if t == 1:
            half_arrived(z * 2 + oy, 0)
            half_arrived(z * 2 + oy, 1)
            add_block(z * 2 + oy)
        else:
            add_pair(t - 1, oy, True)
    add_pair(nz - 1, oy, True)

    mate = chip * 2 + oc
    before = len(pending)
    for i in range(chips):
        to = lax.rem(chip + 1 + i, chips)
        zsend[to] = acc[pl.ds((to * 2 + oc) * rows, rows), :].astype(BF16)
        send(zsend.at[to], s1_recv.at[to], s1_sems.at[0, to], s1_sems.at[1, to], blk, mate)
    total = None
    for i in range(chips):
        to = lax.rem(chip + 1 + i, chips)
        arrived(s1_recv.at[to], s1_sems.at[0, 0], s1_sems.at[1, to])
        part = acc[pl.ds((to * 2 + core) * rows, rows), :] + s1_recv[to].astype(F32)
        if i < chips - 1:
            ysend[to] = part.astype(BF16)
            send(
                ysend.at[to],
                s2_recv.at[chip],
                s2_sems.at[0, to],
                s2_sems.at[1, chip],
                blk,
                to * 2 + core,
            )
        else:
            total = part
    for i in range(chips - 1):
        frm = lax.rem(chip + 1 + i, chips)
        arrived(s2_recv.at[frm], s2_sems.at[0, 0], s2_sems.at[1, frm])
        total = total + s2_recv[frm].astype(F32)
    agg = total.astype(BF16)
    rep_sends = len(pending)

    zvals = zself[...] + dot_nn(agg, wn_ref[...])
    sig = jax.nn.sigmoid(zvals)
    out_ref[...] = (zvals * sig).astype(BF16)
    dz = (cot_ref[...].astype(F32) * sig * (1.0 + zvals * (1.0 - sig))).astype(BF16)
    fhalf = width // 2

    def pass_dg(q, h, at, to):
        half_of = dg.at[q, pl.ds(h * fhalf, fhalf)]
        send(half_of, half_of, dg_ssem.at[at, h], dg_rsem.at[q, h], blk, to)

    def dg_arrived(q, h):
        arrived(dg.at[q, pl.ds(h * fhalf, fhalf)], dg_ssem.at[0, 0], dg_rsem.at[q, h])

    for h in range(2):
        at = slice(h * fhalf, (h + 1) * fhalf)
        dg[rep, at, :] = dot_nt(wn_ref[at, :], dz).astype(BF16)
        for i in range(chips - 1):
            pass_dg(rep, h, i, lax.rem(chip + 1 + i, chips) * 2 + core)
        pass_dg(rep, h, chips, mate)

    gown[0] = dot_tn(x_ref[...], dz)
    gown[1] = dot_tn(agg, dz)
    gbias = jnp.broadcast_to(jnp.sum(dz.astype(F32), axis=0, keepdims=True), (PAD, width))
    ga_send[0:width, :] = gown[oc].astype(BF16)
    ga_send[width : width + PAD, :] = gbias.astype(BF16)
    send(ga_send, ga_recv, ga_sems.at[0], ga_sems.at[1], blk, mate)
    own = dot_nt(dz, ws_ref[...])
    piece = width // nblk

    def pass_chips_dg(h):
        for i in range(chips - 1):
            frm = lax.rem(chip + 1 + i, chips) * 2 + core
            dg_arrived(frm, h)
            pass_dg(frm, h, chips + 1 + i, mate)

    pass_chips_dg(0)

    arrived(ga_recv, ga_sems.at[0], ga_sems.at[1])
    gbias = gbias.astype(BF16).astype(F32) + ga_recv[width : width + PAD, :].astype(F32)
    gown[0] = gown[core] + ga_recv[0:width, :].astype(F32)
    for b in range(nblk):
        gc_send[b, 0:piece, :] = gown[0, b * piece : (b + 1) * piece].astype(BF16)
        gc_send[b, piece : piece + PAD, :] = gbias.astype(BF16)
    gc_buf[blk] = gc_send[blk]
    for i in range(1, nblk):
        to = lax.rem(blk + i, nblk)
        send(gc_send.at[to], gc_buf.at[blk], gc_sems.at[0, to], gc_sems.at[1, blk], to, rep)

    pass_chips_dg(1)

    for _, copy in pending[before:rep_sends]:
        copy.wait_send()
    del pending[before:rep_sends]

    def term(c, lo=0, count=width):
        if nrep <= 4:
            out = dot_nn(dg[0, lo : lo + count], dense[c, 0:rows, :])
            for q in range(1, nrep):
                out = out + dot_nn(
                    dg[q, lo : lo + count], dense[c, q * rows : (q + 1) * rows, :]
                )
            return out

        def step(q, out):
            return out + dot_nn(dg[q, lo : lo + count], dense[c, pl.ds(q * rows, rows), :])

        return lax.fori_loop(0, nrep, step, jnp.zeros((count, rows), F32))

    def y_copy(dest, h):
        at = pl.ds(h * fhalf, fhalf)
        return pltpu.make_async_remote_copy(
            src_ref=ysend.at[dest, at],
            dst_ref=yrecv.at[dest, at],
            send_sem=y_sems.at[0, dest, h],
            recv_sem=y_sems.at[1, dest, h],
            device_id=(z * 2 + oy, rep),
            device_id_type=MESH,
        )

    def grad_blocks():
        for i in range(1, nblk):
            frm = lax.rem(blk + i, nblk)
            arrived(gc_buf.at[frm], gc_sems.at[0, 0], gc_sems.at[1, frm])
        tot = gc_buf[0].astype(F32)
        for b in range(1, nblk):
            tot = tot + gc_buf[b].astype(F32)
        gb_buf[chip] = tot.astype(BF16)
        for i in range(chips - 1):
            to = lax.rem(chip + 1 + i, chips)
            send(
                gb_buf.at[chip],
                gb_buf.at[chip],
                gb_sems.at[0, i],
                gb_sems.at[1, chip],
                blk,
                to * 2 + core,
            )

    def grad_chips():
        for i in range(chips - 1):
            frm = lax.rem(chip + 1 + i, chips)
            arrived(gb_buf.at[frm], gb_sems.at[0, 0], gb_sems.at[1, frm])
        tot = gb_buf[0].astype(F32)
        for i in range(1, chips):
            tot = tot + gb_buf[i].astype(F32)
        gb_ref[...] = tot[piece : piece + 1]
        here = ge_buf.at[core, pl.ds(blk * piece, piece)]
        ge_buf[core, pl.ds(blk * piece, piece), :] = tot[0:piece].astype(BF16)
        for i in range(1, nblk):
            to = lax.rem(blk + i, nblk)
            send(here, here, gd_sems.at[0, to], gd_sems.at[1, blk], to, rep)

    near = jnp.minimum(z, nz - 1 - z)

    def y_dest(i):
        dest = jnp.where(
            i < 2 * near,
            jnp.where(lax.rem(i, 2) == 0, nz - 1 - i // 2, i // 2),
            nz - 1 - (i - near),
        )
        return jnp.where(z < nz // 2, dest, nz - 1 - dest)

    def send_y(i, carry):
        dest = y_dest(i)
        ysend[dest] = term(dest * 2 + oy).astype(BF16)
        y_copy(dest, 0).start()
        y_copy(dest, 1).start()
        return carry

    far = y_dest(jnp.int32(0))
    for h in range(2):
        for i in range(chips):
            dg_arrived(lax.rem(chip + i, chips) * 2 + oc, h)
        at = slice(h * fhalf, (h + 1) * fhalf)
        ysend[far, at, :] = term(far * 2 + oy, h * fhalf, fhalf).astype(BF16)
        y_copy(far, h).start()
    lax.fori_loop(1, nz, send_y, 0)
    grad_blocks()

    def own_term(i, carry):
        acc[pl.ds(i * width, width), :] = term(i * 2 + y)
        return carry

    lax.fori_loop(0, nz, own_term, 0)

    def grad_back():
        for i in range(1, nblk):
            frm = lax.rem(blk + i, nblk)
            arrived(
                ge_buf.at[core, pl.ds(frm * piece, piece)], gd_sems.at[0, 0], gd_sems.at[1, frm]
            )
        send(ge_buf.at[core], ge_buf.at[core], gf_sems.at[0], gf_sems.at[1], blk, mate)

    def add_from(buf, dest, h, sem):
        at = pl.ds(dest * width + h * fhalf, fhalf)
        arrived(buf.at[pl.ds(h * fhalf, fhalf)], z_ssem.at[0, 0], sem)
        acc[at, :] += buf[h * fhalf : (h + 1) * fhalf, :].astype(F32)

    def chain(k, way, cond):
        dest = nz - 1 - k if way == 0 else k
        on = blk + 2 if way == 0 else blk - 2
        more = z > 0 if way == 0 else z < nz - 1
        cond = jnp.logical_and(cond, z < dest if way == 0 else z > dest)
        for h in range(2):

            @pl.when(cond)
            def _():
                add_from(yrecv.at[dest], dest, h, y_sems.at[1, dest, h])

                @pl.when(more)
                def _():
                    add_from(zrecv.at[way, dest], dest, h, z_rsem.at[way, dest, h])

                rows_at = pl.ds(dest * width + h * fhalf, fhalf)
                zsend[dest, h * fhalf : (h + 1) * fhalf, :] = acc[rows_at, :].astype(BF16)

            at = pl.ds(h * fhalf, fhalf)
            send(
                zsend.at[dest, at],
                zrecv.at[way, dest, at],
                z_ssem.at[dest, h],
                z_rsem.at[way, dest, h],
                on,
                rep,
                cond,
            )

    at_end = near == 0
    chain(0, 0, z == 0)
    chain(0, 1, z == nz - 1)
    grad_chips()
    for k in range(nz - 1):
        inside = z >= 0 if k else jnp.logical_not(at_end)
        chain(k, 0, jnp.logical_and(inside, z < nz // 2))
        chain(k, 1, inside)
        chain(k, 0, jnp.logical_and(inside, z >= nz // 2))

    grad_back()
    for h in range(2):
        add_from(yrecv.at[z], z, h, y_sems.at[1, z, h])

        @pl.when(z > 0)
        def _():
            add_from(zrecv.at[0, z], z, h, z_rsem.at[0, z, h])

        @pl.when(z < nz - 1)
        def _():
            add_from(zrecv.at[1, z], z, h, z_rsem.at[1, z, h])

    gradf_ref[...] = (own + acc[pl.ds(z * width, width), :].T).astype(BF16)

    arrived(ge_buf.at[oc], gf_sems.at[0], gf_sems.at[1])
    ge_ref[...] = ge_buf[...]

    for cond, copy in pending:
        if cond is None:
            copy.wait_send()
        else:
            pl.when(cond)(copy.wait_send)

    def drain_y(i, carry):
        y_copy(i, 0).wait_send()
        y_copy(i, 1).wait_send()
        return carry

    lax.fori_loop(0, nz, drain_y, 0)


def hand_out(a_ref, b_ref, c_ref, d_ref, out_ref, gradf_ref, gs_ref, gn_ref, gb_ref):
    out_ref[...] = a_ref[...]
    gradf_ref[...] = b_ref[...]
    gs_ref[...] = c_ref[0].astype(F32)
    gn_ref[...] = c_ref[1].astype(F32)
    gb_ref[...] = d_ref[...]


def local(
    features, w_self, w_neigh, bias, cotangent, tile_values, tile_rows, tile_cols, tile_counts
):
    rows, width = features.shape
    nblk, nrep = lax.axis_size("blk"), lax.axis_size("rep")
    slots, tile = tile_values.shape[3], tile_values.shape[4]
    per_dev = rows // tile
    lanes = max(128, nrep * per_dev * per_dev)
    nz, chips = nblk // 2, nrep // 2
    piece = width // nblk

    cfg = (nblk, nrep, slots, tile, rows, width)
    vmem = pl.BlockSpec(memory_space=pltpu.VMEM)
    sems = pltpu.SemaphoreType.DMA
    outs = pl.pallas_call(
        functools.partial(kernel, cfg),
        out_shape=(
            jax.ShapeDtypeStruct((rows, width), BF16),
            jax.ShapeDtypeStruct((rows, width), BF16),
            jax.ShapeDtypeStruct((2, width, width), BF16),
            jax.ShapeDtypeStruct((1, width), F32),
        ),
        in_specs=[
            pl.BlockSpec(memory_space=pltpu.SMEM),
            vmem,
            vmem,
            vmem,
            vmem,
            vmem,
            vmem,
            vmem,
            pl.BlockSpec(memory_space=pl.ANY),
        ],
        out_specs=(vmem,) * 4,
        scratch_shapes=[
            pltpu.VMEM((nblk * slots + 1, tile, tile), BF16),
            pltpu.VMEM((nblk, nrep * rows, rows), BF16),
            pltpu.VMEM((nblk, rows, width), BF16),
            pltpu.VMEM((max(nrep * rows, nz * width), width), F32),
            pltpu.VMEM((rows, width), F32),
            pltpu.VMEM((max(chips, nz), rows, width), BF16),
            pltpu.VMEM((chips, rows, width), BF16),
            pltpu.VMEM((max(chips, nz), rows, width), BF16),
            pltpu.VMEM((chips, rows, width), BF16),
            pltpu.VMEM((nrep, width, rows), BF16),
                pltpu.VMEM((nz, width, rows), BF16),
            pltpu.VMEM((2, nz, width, rows), BF16),
            pltpu.VMEM((2, width, width), F32),
            pltpu.VMEM((width + PAD, width), BF16),
            pltpu.VMEM((width + PAD, width), BF16),
            pltpu.VMEM((chips, piece + PAD, width), BF16),
            pltpu.VMEM((nblk, piece + PAD, width), BF16),
            pltpu.VMEM((nblk, piece + PAD, width), BF16),
            pltpu.VMEM((2, width, width), BF16),
            pltpu.VMEM((nblk, lanes), jnp.int32),
            pltpu.SMEM((nblk, lanes), jnp.int32),
            sems,
            sems,
            sems((nblk, 2)),
            sems((nz, 2, 4)),
            sems((2, chips)),
            sems((2, chips)),
            sems((nrep, 2)),
            sems((2 * chips + 1, 2)),
            sems((2, nz, 2)),
            sems((nz, 2)),
            sems((2, nz, 2)),
            sems((2,)),
            sems((2, chips)),
            sems((2, nblk)),
            sems((2, nblk)),
            sems((2,)),
        ],
        compiler_params=pltpu.CompilerParams(
            collective_id=0, has_side_effects=True, vmem_limit_bytes=60 * 1024 * 1024
        ),
        cost_estimate=pl.CostEstimate(
            flops=4 * nblk * nrep * rows * rows * width,
            bytes_accessed=nblk * slots * tile * tile * 2,
            transcendentals=rows * width,
        ),
    )(
        tile_counts.reshape(1, nblk),
        tile_rows.reshape(nblk, slots),
        tile_cols.reshape(nblk, slots),
        features,
        w_self,
        w_neigh,
        bias.reshape(1, width),
        cotangent,
        tile_values.reshape(nblk * slots, tile, tile),
    )
    output, grad_features, grad_self, grad_neigh, grad_bias = pl.pallas_call(
        hand_out,
        out_shape=(
            jax.ShapeDtypeStruct((rows, width), BF16),
            jax.ShapeDtypeStruct((rows, width), BF16),
            jax.ShapeDtypeStruct((width, width), F32),
            jax.ShapeDtypeStruct((width, width), F32),
            jax.ShapeDtypeStruct((1, width), F32),
        ),
        in_specs=[vmem] * 4,
        out_specs=(vmem,) * 5,
    )(*outs)
    return output, grad_features, grad_self, grad_neigh, grad_bias.reshape(width)


def solution(mesh):
    in_specs = (
        P(("blk", "rep"), None),
        P(),
        P(),
        P(),
        P(("blk", "rep"), None),
        P("blk", "rep", None, None, None, None),
        P("blk", "rep", None, None),
        P("blk", "rep", None, None),
        P("blk", "rep", None),
    )
    out_specs = (P(("blk", "rep"), None), P(("blk", "rep"), None), P(), P(), P())
    return jax.shard_map(local, mesh=mesh, in_specs=in_specs, out_specs=out_specs, check_vma=False)
```

```python
import functools

import jax
import jax.numpy as jnp
from jax import lax
from jax.experimental import pallas as pl
from jax.experimental.pallas import tpu as pltpu
from jax.sharding import PartitionSpec as P

MESH = pl.DeviceIdType.MESH
F32 = jnp.float32
BF16 = jnp.bfloat16
PAD = 16


def dot_nn(a, b):
    return jnp.dot(a, b, preferred_element_type=F32)


def dot_nt(a, b):
    return lax.dot_general(a, b, (((1,), (1,)), ((), ())), preferred_element_type=F32)


def dot_tn(a, b):
    return lax.dot_general(a, b, (((0,), (0,)), ((), ())), preferred_element_type=F32)


def kernel(
    cfg,
    counts_ref,
    trows_ref,
    tcols_ref,
    x_ref,
    ws_ref,
    wn_ref,
    bias_ref,
    cot_ref,
    values_ref,
    out_ref,
    gradf_ref,
    ge_ref,
    gb_ref,
    vals,
    dense,
    xg,
    acc,
    zself,
    zsend,
    s1_recv,
    ysend,
    s2_recv,
    dg,
    yrecv,
    zrecv,
    gown,
    ga_send,
    ga_recv,
    gb_buf,
    gc_buf,
    gc_send,
    ge_buf,
    place_vec,
    place_ref,
    vals_sem,
    place_sem,
    x_rsem,
    x_ssem,
    s1_sems,
    s2_sems,
    dg_rsem,
    dg_ssem,
    y_sems,
    z_ssem,
    z_rsem,
    ga_sems,
    gb_sems,
    gc_sems,
    gd_sems,
    gf_sems,
):
    nblk, nrep, slots, tile, rows, width = cfg
    nz, chips = nblk // 2, nrep // 2
    per_dev = rows // tile
    rtiles = nrep * per_dev
    blk = lax.axis_index("blk")
    rep = lax.axis_index("rep")
    z, y = blk // 2, lax.rem(blk, 2)
    chip, core = rep // 2, lax.rem(rep, 2)
    oy, oc = 1 - y, 1 - core

    pending = []

    def send(src, dst, ssem, rsem, to_blk, to_rep, cond=None):
        copy = pltpu.make_async_remote_copy(
            src_ref=src,
            dst_ref=dst,
            send_sem=ssem,
            recv_sem=rsem,
            device_id=(to_blk, to_rep),
            device_id_type=MESH,
        )
        if cond is None:
            copy.start()
        else:
            pl.when(cond)(copy.start)
        pending.append((cond, copy))

    def arrived(dst, ssem, rsem):
        pltpu.make_async_remote_copy(
            src_ref=dst,
            dst_ref=dst,
            send_sem=ssem,
            recv_sem=rsem,
            device_id=(blk, rep),
            device_id_type=MESH,
        ).wait_recv()

    load = pltpu.make_async_copy(values_ref, vals.at[pl.ds(0, nblk * slots)], vals_sem)
    load.start()

    lanes = place_vec.shape[1]
    row_at = lax.broadcasted_iota(jnp.int32, (nblk, lanes), 0)
    lane = lax.broadcasted_iota(jnp.int32, (nblk, lanes), 1)

    def find_places():
        live = jnp.zeros((nblk, lanes), jnp.int32)
        for c in range(nblk):
            live = jnp.where(row_at == c, counts_ref[0, c], live)
        at = trows_ref[...] * per_dev + tcols_ref[...]
        found = jnp.full((nblk, lanes), nblk * slots, jnp.int32)
        for slot in range(slots):
            hit = jnp.logical_and(at[:, slot : slot + 1] == lane, live > slot)
            found = jnp.where(hit, row_at * slots + slot, found)
        place_vec[...] = found
        move = pltpu.make_async_copy(place_vec, place_ref, place_sem)
        move.start()
        return move

    barrier = pltpu.get_barrier_semaphore()
    for i in range(1, nblk):
        pl.semaphore_signal(
            barrier, inc=1, device_id=(lax.rem(blk + i, nblk), rep), device_id_type=MESH
        )
    for i in range(1, nrep):
        pl.semaphore_signal(
            barrier, inc=1, device_id=(blk, lax.rem(rep + i, nrep)), device_id_type=MESH
        )
    pl.semaphore_wait(barrier, nblk + nrep - 2)

    fhalf = width // 2

    def pass_on(origin, step, h, kind, to_blk, cond):
        held = xg.at[origin, h]
        send(held, held, x_ssem.at[step, h, kind], x_rsem.at[origin, h], to_blk, rep, cond)

    for h in range(2):
        xg[blk, h] = x_ref[:, h * fhalf : (h + 1) * fhalf]
        pass_on(blk, 0, h, 0, blk + 2, z < nz - 1)
        pass_on(blk, 0, h, 1, blk - 2, z > 0)
        pass_on(blk, 0, h, 2, z * 2 + oy, None)

    move = find_places()
    zself[...] = dot_nn(x_ref[...], ws_ref[...]) + bias_ref[...]
    vals[nblk * slots] = jnp.zeros((tile, tile), BF16)
    move.wait()
    load.wait()

    def place_tiles(c, carry):
        def place_row(r):
            for t in range(per_dev):
                dense[c, pl.ds(r * tile, tile), t * tile : (t + 1) * tile] = vals[
                    place_ref[c, r * per_dev + t]
                ]

        if rtiles <= 8:
            for r in range(rtiles):
                place_row(r)
        else:
            pl.loop(0, rtiles)(place_row)
        return carry

    lax.fori_loop(0, nblk, place_tiles, 0)

    chunk = nrep * rows if nrep <= 4 else rows

    def add_block(c, h, first=False):
        def part(i):
            at = pl.ds(i * chunk, chunk)
            prod = dot_nn(dense[c, at, :], xg[c, h])
            if first:
                acc[at, h * fhalf : (h + 1) * fhalf] = prod
            else:
                acc[at, h * fhalf : (h + 1) * fhalf] += prod

        count = nrep * rows // chunk
        if count == 1:
            part(0)
        else:
            pl.loop(0, count)(part)

    def x_arrived(origin, h):
        arrived(xg.at[origin, h], x_ssem.at[0, 0, 0], x_rsem.at[origin, h])

    def add_column(step, h):
        for at in (z - step, z + step):

            @pl.when(jnp.logical_and(at >= 0, at < nz))
            def _():
                add_block(at * 2 + y, h)

    def add_across(step, h):
        for at in (z - step, z + step)[: 2 if step else 1]:
            origin = at * 2 + oy

            @pl.when(jnp.logical_and(at >= 0, at < nz))
            def _():
                x_arrived(origin, h)
                add_block(origin, h)

    def relay(t, h):
        for at, kind, inner in ((z - t, 0, z < nz - 1), (z + t, 1, z > 0)):
            origin = at * 2 + y
            there = at >= 0 if kind == 0 else at < nz
            on = blk + 2 if kind == 0 else blk - 2

            @pl.when(there)
            def _():
                x_arrived(origin, h)

            pass_on(origin, t, h, kind, on, jnp.logical_and(there, inner))
            pass_on(origin, t, h, kind + 2, z * 2 + oy, there)

    mate = chip * 2 + oc
    rep_sends = []

    def cores_send(h):
        cols = pl.ds(h * fhalf, fhalf)
        start = len(pending)
        for i in range(chips):
            to = lax.rem(chip + 1 + i, chips)
            zsend[to, :, h * fhalf : (h + 1) * fhalf] = acc[
                pl.ds((to * 2 + oc) * rows, rows), h * fhalf : (h + 1) * fhalf
            ].astype(BF16)
            send(
                zsend.at[to, :, cols],
                s1_recv.at[to, :, cols],
                s1_sems.at[0, to, h],
                s1_sems.at[1, to, h],
                blk,
                mate,
            )
        rep_sends.extend(pending[start:])
        del pending[start:]

    def cores_sum(h):
        cols = pl.ds(h * fhalf, fhalf)
        at = slice(h * fhalf, (h + 1) * fhalf)
        start = len(pending)
        total = None
        for i in range(chips):
            to = lax.rem(chip + 1 + i, chips)
            arrived(s1_recv.at[to, :, cols], s1_sems.at[0, 0, 0], s1_sems.at[1, to, h])
            total = acc[pl.ds((to * 2 + core) * rows, rows), at] + s1_recv[to, :, at].astype(F32)
            if i < chips - 1:
                ysend[to, :, at] = total.astype(BF16)
                send(
                    ysend.at[to, :, cols],
                    s2_recv.at[chip, :, cols],
                    s2_sems.at[0, to, h],
                    s2_sems.at[1, chip, h],
                    blk,
                    to * 2 + core,
                )
        acc[pl.ds((chip * 2 + core) * rows, rows), at] = total
        rep_sends.extend(pending[start:])
        del pending[start:]

    def chips_sum(h):
        cols = pl.ds(h * fhalf, fhalf)
        at = slice(h * fhalf, (h + 1) * fhalf)
        total = acc[pl.ds((chip * 2 + core) * rows, rows), at]
        for i in range(chips - 1):
            frm = lax.rem(chip + 1 + i, chips)
            arrived(s2_recv.at[frm, :, cols], s2_sems.at[0, 0, 0], s2_sems.at[1, frm, h])
            total = total + s2_recv[frm, :, at].astype(F32)
        return total.astype(BF16)

    add_block(blk, 0, True)
    add_block(blk, 1, True)
    relay(1, 0)
    relay(1, 1)
    for t in range(2, nz):
        add_column(t - 1, 0)
        relay(t, 0)
        add_across(t - 2, 0)
    add_column(nz - 1, 0)
    for t in range(2, nz):
        relay(t, 1)
        add_column(t - 1, 1)
        if t == 2:
            add_across(nz - 2, 0)
    add_across(nz - 1, 0)
    cores_send(0)
    add_column(nz - 1, 1)
    add_across(0, 1)
    add_across(1, 1)
    cores_sum(0)
    for t in range(2, nz):
        add_across(t, 1)
    cores_send(1)
    cores_sum(1)
    agg0 = chips_sum(0)
    zpart = zself[...] + dot_nn(agg0, wn_ref[0:fhalf, :])
    agg1 = chips_sum(1)

    agg = jnp.concatenate([agg0, agg1], axis=1)
    zvals = zpart + dot_nn(agg1, wn_ref[fhalf:width, :])
    sig = jax.nn.sigmoid(zvals)
    out_ref[...] = (zvals * sig).astype(BF16)
    dz = (cot_ref[...].astype(F32) * sig * (1.0 + zvals * (1.0 - sig))).astype(BF16)
    def pass_dg(q, h, at, to):
        half_of = dg.at[q, pl.ds(h * fhalf, fhalf)]
        send(half_of, half_of, dg_ssem.at[at, h], dg_rsem.at[q, h], blk, to)

    def dg_arrived(q, h):
        arrived(dg.at[q, pl.ds(h * fhalf, fhalf)], dg_ssem.at[0, 0], dg_rsem.at[q, h])

    for h in range(2):
        at = slice(h * fhalf, (h + 1) * fhalf)
        dg[rep, at, :] = dot_nt(wn_ref[at, :], dz).astype(BF16)
        for i in range(chips - 1):
            pass_dg(rep, h, i, lax.rem(chip + 1 + i, chips) * 2 + core)
        pass_dg(rep, h, chips, mate)

    gown[0] = dot_tn(x_ref[...], dz)
    gown[1] = dot_tn(agg, dz)
    gbias = jnp.broadcast_to(jnp.sum(dz.astype(F32), axis=0, keepdims=True), (PAD, width))
    ga_send[0:width, :] = gown[oc].astype(BF16)
    ga_send[width : width + PAD, :] = gbias.astype(BF16)
    send(ga_send, ga_recv, ga_sems.at[0], ga_sems.at[1], blk, mate)
    own = dot_nt(dz, ws_ref[...])
    piece = width // nblk

    def pass_chips_dg(h):
        for i in range(chips - 1):
            frm = lax.rem(chip + 1 + i, chips) * 2 + core
            dg_arrived(frm, h)
            pass_dg(frm, h, chips + 1 + i, mate)

    pass_chips_dg(0)

    arrived(ga_recv, ga_sems.at[0], ga_sems.at[1])
    gbias = gbias.astype(BF16).astype(F32) + ga_recv[width : width + PAD, :].astype(F32)
    gown[0] = gown[core] + ga_recv[0:width, :].astype(F32)
    for b in range(nblk):
        gc_send[b, 0:piece, :] = gown[0, b * piece : (b + 1) * piece].astype(BF16)
        gc_send[b, piece : piece + PAD, :] = gbias.astype(BF16)
    gc_buf[blk] = gc_send[blk]
    for i in range(1, nblk):
        to = lax.rem(blk + i, nblk)
        send(gc_send.at[to], gc_buf.at[blk], gc_sems.at[0, to], gc_sems.at[1, blk], to, rep)

    pass_chips_dg(1)

    for _, copy in rep_sends:
        copy.wait_send()

    def term(c, lo=0, count=width):
        if nrep <= 4:
            out = dot_nn(dg[0, lo : lo + count], dense[c, 0:rows, :])
            for q in range(1, nrep):
                out = out + dot_nn(
                    dg[q, lo : lo + count], dense[c, q * rows : (q + 1) * rows, :]
                )
            return out

        def step(q, out):
            return out + dot_nn(dg[q, lo : lo + count], dense[c, pl.ds(q * rows, rows), :])

        return lax.fori_loop(0, nrep, step, jnp.zeros((count, rows), F32))

    def y_copy(dest, h):
        at = pl.ds(h * fhalf, fhalf)
        return pltpu.make_async_remote_copy(
            src_ref=ysend.at[dest, at],
            dst_ref=yrecv.at[dest, at],
            send_sem=y_sems.at[0, dest, h],
            recv_sem=y_sems.at[1, dest, h],
            device_id=(z * 2 + oy, rep),
            device_id_type=MESH,
        )

    def grad_blocks():
        for i in range(1, nblk):
            frm = lax.rem(blk + i, nblk)
            arrived(gc_buf.at[frm], gc_sems.at[0, 0], gc_sems.at[1, frm])
        tot = gc_buf[0].astype(F32)
        for b in range(1, nblk):
            tot = tot + gc_buf[b].astype(F32)
        gb_buf[chip] = tot.astype(BF16)
        for i in range(chips - 1):
            to = lax.rem(chip + 1 + i, chips)
            send(
                gb_buf.at[chip],
                gb_buf.at[chip],
                gb_sems.at[0, i],
                gb_sems.at[1, chip],
                blk,
                to * 2 + core,
            )

    def grad_chips():
        for i in range(chips - 1):
            frm = lax.rem(chip + 1 + i, chips)
            arrived(gb_buf.at[frm], gb_sems.at[0, 0], gb_sems.at[1, frm])
        tot = gb_buf[0].astype(F32)
        for i in range(1, chips):
            tot = tot + gb_buf[i].astype(F32)
        gb_ref[...] = tot[piece : piece + 1]
        here = ge_buf.at[core, pl.ds(blk * piece, piece)]
        ge_buf[core, pl.ds(blk * piece, piece), :] = tot[0:piece].astype(BF16)
        for i in range(1, nblk):
            to = lax.rem(blk + i, nblk)
            send(here, here, gd_sems.at[0, to], gd_sems.at[1, blk], to, rep)

    near = jnp.minimum(z, nz - 1 - z)

    def y_dest(i):
        dest = jnp.where(
            i < 2 * near,
            jnp.where(lax.rem(i, 2) == 0, nz - 1 - i // 2, i // 2),
            nz - 1 - (i - near),
        )
        return jnp.where(z < nz // 2, dest, nz - 1 - dest)

    def send_y(i, carry):
        dest = y_dest(i)
        ysend[dest] = term(dest * 2 + oy).astype(BF16)
        y_copy(dest, 0).start()
        y_copy(dest, 1).start()
        return carry

    far = y_dest(jnp.int32(0))
    for h in range(2):
        for i in range(chips):
            dg_arrived(lax.rem(chip + i, chips) * 2 + oc, h)
        at = slice(h * fhalf, (h + 1) * fhalf)
        ysend[far, at, :] = term(far * 2 + oy, h * fhalf, fhalf).astype(BF16)
        y_copy(far, h).start()
    lax.fori_loop(1, nz, send_y, 0)
    grad_blocks()

    def own_term(i, carry):
        acc[pl.ds(i * width, width), :] = term(i * 2 + y)
        return carry

    lax.fori_loop(0, nz, own_term, 0)

    def grad_back():
        for i in range(1, nblk):
            frm = lax.rem(blk + i, nblk)
            arrived(
                ge_buf.at[core, pl.ds(frm * piece, piece)], gd_sems.at[0, 0], gd_sems.at[1, frm]
            )
        send(ge_buf.at[core], ge_buf.at[core], gf_sems.at[0], gf_sems.at[1], blk, mate)

    def add_from(buf, dest, h, sem):
        at = pl.ds(dest * width + h * fhalf, fhalf)
        arrived(buf.at[pl.ds(h * fhalf, fhalf)], z_ssem.at[0, 0], sem)
        acc[at, :] += buf[h * fhalf : (h + 1) * fhalf, :].astype(F32)

    def chain(k, way, cond):
        dest = nz - 1 - k if way == 0 else k
        on = blk + 2 if way == 0 else blk - 2
        more = z > 0 if way == 0 else z < nz - 1
        cond = jnp.logical_and(cond, z < dest if way == 0 else z > dest)
        for h in range(2):

            @pl.when(cond)
            def _():
                add_from(yrecv.at[dest], dest, h, y_sems.at[1, dest, h])

                @pl.when(more)
                def _():
                    add_from(zrecv.at[way, dest], dest, h, z_rsem.at[way, dest, h])

                rows_at = pl.ds(dest * width + h * fhalf, fhalf)
                zsend[dest, h * fhalf : (h + 1) * fhalf, :] = acc[rows_at, :].astype(BF16)

            at = pl.ds(h * fhalf, fhalf)
            send(
                zsend.at[dest, at],
                zrecv.at[way, dest, at],
                z_ssem.at[dest, h],
                z_rsem.at[way, dest, h],
                on,
                rep,
                cond,
            )

    at_end = near == 0
    chain(0, 0, z == 0)
    chain(0, 1, z == nz - 1)
    grad_chips()
    for k in range(nz - 1):
        inside = z >= 0 if k else jnp.logical_not(at_end)
        chain(k, 0, jnp.logical_and(inside, z < nz // 2))
        chain(k, 1, inside)
        chain(k, 0, jnp.logical_and(inside, z >= nz // 2))

    grad_back()
    for h in range(2):
        add_from(yrecv.at[z], z, h, y_sems.at[1, z, h])

        @pl.when(z > 0)
        def _():
            add_from(zrecv.at[0, z], z, h, z_rsem.at[0, z, h])

        @pl.when(z < nz - 1)
        def _():
            add_from(zrecv.at[1, z], z, h, z_rsem.at[1, z, h])

    gradf_ref[...] = (own + acc[pl.ds(z * width, width), :].T).astype(BF16)

    arrived(ge_buf.at[oc], gf_sems.at[0], gf_sems.at[1])
    ge_ref[...] = ge_buf[...]

    for cond, copy in pending:
        if cond is None:
            copy.wait_send()
        else:
            pl.when(cond)(copy.wait_send)

    def drain_y(i, carry):
        y_copy(i, 0).wait_send()
        y_copy(i, 1).wait_send()
        return carry

    lax.fori_loop(0, nz, drain_y, 0)


def hand_out(a_ref, b_ref, c_ref, d_ref, out_ref, gradf_ref, gs_ref, gn_ref, gb_ref):
    out_ref[...] = a_ref[...]
    gradf_ref[...] = b_ref[...]
    gs_ref[...] = c_ref[0].astype(F32)
    gn_ref[...] = c_ref[1].astype(F32)
    gb_ref[...] = d_ref[...]


def local(
    features, w_self, w_neigh, bias, cotangent, tile_values, tile_rows, tile_cols, tile_counts
):
    rows, width = features.shape
    nblk, nrep = lax.axis_size("blk"), lax.axis_size("rep")
    slots, tile = tile_values.shape[3], tile_values.shape[4]
    per_dev = rows // tile
    lanes = max(128, nrep * per_dev * per_dev)
    nz, chips = nblk // 2, nrep // 2
    piece = width // nblk

    cfg = (nblk, nrep, slots, tile, rows, width)
    vmem = pl.BlockSpec(memory_space=pltpu.VMEM)
    sems = pltpu.SemaphoreType.DMA
    outs = pl.pallas_call(
        functools.partial(kernel, cfg),
        out_shape=(
            jax.ShapeDtypeStruct((rows, width), BF16),
            jax.ShapeDtypeStruct((rows, width), BF16),
            jax.ShapeDtypeStruct((2, width, width), BF16),
            jax.ShapeDtypeStruct((1, width), F32),
        ),
        in_specs=[
            pl.BlockSpec(memory_space=pltpu.SMEM),
            vmem,
            vmem,
            vmem,
            vmem,
            vmem,
            vmem,
            vmem,
            pl.BlockSpec(memory_space=pl.ANY),
        ],
        out_specs=(vmem,) * 4,
        scratch_shapes=[
            pltpu.VMEM((nblk * slots + 1, tile, tile), BF16),
            pltpu.VMEM((nblk, nrep * rows, rows), BF16),
            pltpu.VMEM((nblk, 2, rows, width // 2), BF16),
            pltpu.VMEM((max(nrep * rows, nz * width), width), F32),
            pltpu.VMEM((rows, width), F32),
            pltpu.VMEM((max(chips, nz), rows, width), BF16),
            pltpu.VMEM((chips, rows, width), BF16),
            pltpu.VMEM((max(chips, nz), rows, width), BF16),
            pltpu.VMEM((chips, rows, width), BF16),
            pltpu.VMEM((nrep, width, rows), BF16),
                pltpu.VMEM((nz, width, rows), BF16),
            pltpu.VMEM((2, nz, width, rows), BF16),
            pltpu.VMEM((2, width, width), F32),
            pltpu.VMEM((width + PAD, width), BF16),
            pltpu.VMEM((width + PAD, width), BF16),
            pltpu.VMEM((chips, piece + PAD, width), BF16),
            pltpu.VMEM((nblk, piece + PAD, width), BF16),
            pltpu.VMEM((nblk, piece + PAD, width), BF16),
            pltpu.VMEM((2, width, width), BF16),
            pltpu.VMEM((nblk, lanes), jnp.int32),
            pltpu.SMEM((nblk, lanes), jnp.int32),
            sems,
            sems,
            sems((nblk, 2)),
            sems((nz, 2, 4)),
            sems((2, chips, 2)),
            sems((2, chips, 2)),
            sems((nrep, 2)),
            sems((2 * chips + 1, 2)),
            sems((2, nz, 2)),
            sems((nz, 2)),
            sems((2, nz, 2)),
            sems((2,)),
            sems((2, chips)),
            sems((2, nblk)),
            sems((2, nblk)),
            sems((2,)),
        ],
        compiler_params=pltpu.CompilerParams(
            collective_id=0, has_side_effects=True, vmem_limit_bytes=60 * 1024 * 1024
        ),
        cost_estimate=pl.CostEstimate(
            flops=4 * nblk * nrep * rows * rows * width,
            bytes_accessed=nblk * slots * tile * tile * 2,
            transcendentals=rows * width,
        ),
    )(
        tile_counts.reshape(1, nblk),
        tile_rows.reshape(nblk, slots),
        tile_cols.reshape(nblk, slots),
        features,
        w_self,
        w_neigh,
        bias.reshape(1, width),
        cotangent,
        tile_values.reshape(nblk * slots, tile, tile),
    )
    output, grad_features, grad_self, grad_neigh, grad_bias = pl.pallas_call(
        hand_out,
        out_shape=(
            jax.ShapeDtypeStruct((rows, width), BF16),
            jax.ShapeDtypeStruct((rows, width), BF16),
            jax.ShapeDtypeStruct((width, width), F32),
            jax.ShapeDtypeStruct((width, width), F32),
            jax.ShapeDtypeStruct((1, width), F32),
        ),
        in_specs=[vmem] * 4,
        out_specs=(vmem,) * 5,
    )(*outs)
    return output, grad_features, grad_self, grad_neigh, grad_bias.reshape(width)


def solution(mesh):
    in_specs = (
        P(("blk", "rep"), None),
        P(),
        P(),
        P(),
        P(("blk", "rep"), None),
        P("blk", "rep", None, None, None, None),
        P("blk", "rep", None, None),
        P("blk", "rep", None, None),
        P("blk", "rep", None),
    )
    out_specs = (P(("blk", "rep"), None), P(("blk", "rep"), None), P(), P(), P())
    return jax.shard_map(local, mesh=mesh, in_specs=in_specs, out_specs=out_specs, check_vma=False)
```

```python
import functools

import jax
import jax.numpy as jnp
from jax import lax
from jax.experimental import pallas as pl
from jax.experimental.pallas import tpu as pltpu
from jax.sharding import PartitionSpec as P

MESH = pl.DeviceIdType.MESH
F32 = jnp.float32
BF16 = jnp.bfloat16
PAD = 16


def dot_nn(a, b):
    return jnp.dot(a, b, preferred_element_type=F32)


def dot_nt(a, b):
    return lax.dot_general(a, b, (((1,), (1,)), ((), ())), preferred_element_type=F32)


def dot_tn(a, b):
    return lax.dot_general(a, b, (((0,), (0,)), ((), ())), preferred_element_type=F32)


def kernel(
    cfg,
    counts_ref,
    trows_ref,
    tcols_ref,
    x_ref,
    ws_ref,
    wn_ref,
    bias_ref,
    cot_ref,
    values_ref,
    out_ref,
    gradf_ref,
    ge_ref,
    gb_ref,
    vals,
    dense,
    xg,
    acc,
    zself,
    zsend,
    s1_recv,
    ysend,
    s2_recv,
    dg,
    yrecv,
    zrecv,
    gown,
    ga_send,
    ga_recv,
    gb_buf,
    gc_buf,
    gc_send,
    ge_buf,
    place_vec,
    place_ref,
    vals_sem,
    place_sem,
    x_rsem,
    x_ssem,
    s1_sems,
    s2_sems,
    dg_rsem,
    dg_ssem,
    y_sems,
    z_ssem,
    z_rsem,
    ga_sems,
    gb_sems,
    gc_sems,
    gd_sems,
    gf_sems,
):
    nblk, nrep, slots, tile, rows, width = cfg
    nz, chips = nblk // 2, nrep // 2
    per_dev = rows // tile
    rtiles = nrep * per_dev
    blk = lax.axis_index("blk")
    rep = lax.axis_index("rep")
    z, y = blk // 2, lax.rem(blk, 2)
    chip, core = rep // 2, lax.rem(rep, 2)
    oy, oc = 1 - y, 1 - core

    pending = []

    def send(src, dst, ssem, rsem, to_blk, to_rep, cond=None):
        copy = pltpu.make_async_remote_copy(
            src_ref=src,
            dst_ref=dst,
            send_sem=ssem,
            recv_sem=rsem,
            device_id=(to_blk, to_rep),
            device_id_type=MESH,
        )
        if cond is None:
            copy.start()
        else:
            pl.when(cond)(copy.start)
        pending.append((cond, copy))

    def arrived(dst, ssem, rsem):
        pltpu.make_async_remote_copy(
            src_ref=dst,
            dst_ref=dst,
            send_sem=ssem,
            recv_sem=rsem,
            device_id=(blk, rep),
            device_id_type=MESH,
        ).wait_recv()

    load = pltpu.make_async_copy(values_ref, vals.at[pl.ds(0, nblk * slots)], vals_sem)
    load.start()

    lanes = place_vec.shape[1]
    row_at = lax.broadcasted_iota(jnp.int32, (nblk, lanes), 0)
    lane = lax.broadcasted_iota(jnp.int32, (nblk, lanes), 1)

    def find_places():
        live = jnp.zeros((nblk, lanes), jnp.int32)
        for c in range(nblk):
            live = jnp.where(row_at == c, counts_ref[0, c], live)
        at = trows_ref[...] * per_dev + tcols_ref[...]
        found = jnp.full((nblk, lanes), nblk * slots, jnp.int32)
        for slot in range(slots):
            hit = jnp.logical_and(at[:, slot : slot + 1] == lane, live > slot)
            found = jnp.where(hit, row_at * slots + slot, found)
        place_vec[...] = found
        move = pltpu.make_async_copy(place_vec, place_ref, place_sem)
        move.start()
        return move

    barrier = pltpu.get_barrier_semaphore()
    for i in range(1, nblk):
        pl.semaphore_signal(
            barrier, inc=1, device_id=(lax.rem(blk + i, nblk), rep), device_id_type=MESH
        )
    for i in range(1, nrep):
        pl.semaphore_signal(
            barrier, inc=1, device_id=(blk, lax.rem(rep + i, nrep)), device_id_type=MESH
        )
    pl.semaphore_wait(barrier, nblk + nrep - 2)

    half = rows // 2

    def relay_copy(src, origin, step, h, kind):
        to = (blk + 2, blk - 2, z * 2 + oy, z * 2 + oy)[kind]
        return pltpu.make_async_remote_copy(
            src_ref=src.at[pl.ds(h * half, half)],
            dst_ref=xg.at[origin, pl.ds(h * half, half)],
            send_sem=x_ssem.at[step, h, kind],
            recv_sem=x_rsem.at[origin, h],
            device_id=(to, rep),
            device_id_type=MESH,
        )

    def half_arrived(origin, h):
        arrived(xg.at[origin, pl.ds(h * half, half)], x_ssem.at[0, 0, 0], x_rsem.at[origin, h])

    inner = (z < nz - 1, z > 0)
    for h in range(2):
        pl.when(inner[0])(relay_copy(x_ref, blk, 0, h, 0).start)
        pl.when(inner[1])(relay_copy(x_ref, blk, 0, h, 1).start)
        relay_copy(x_ref, blk, 0, h, 2).start()
    xg[blk] = x_ref[...]

    move = find_places()
    zself[...] = dot_nn(x_ref[...], ws_ref[...]) + bias_ref[...]
    vals[nblk * slots] = jnp.zeros((tile, tile), BF16)
    move.wait()
    load.wait()

    def place_tiles(c, carry):
        def place_row(r):
            for t in range(per_dev):
                dense[c, pl.ds(r * tile, tile), t * tile : (t + 1) * tile] = vals[
                    place_ref[c, r * per_dev + t]
                ]

        if rtiles <= 8:
            for r in range(rtiles):
                place_row(r)
        else:
            pl.loop(0, rtiles)(place_row)
        return carry

    lax.fori_loop(0, nblk, place_tiles, 0)

    chunk = nrep * rows if nrep <= 4 else rows

    def add_block(c):
        def part(i):
            at = pl.ds(i * chunk, chunk)
            acc[at, :] += dot_nn(dense[c, at, :], xg[c])

        count = nrep * rows // chunk
        if count == 1:
            part(0)
        else:
            pl.loop(0, count)(part)

    acc[...] = jnp.zeros_like(acc)

    def gather_step(t, carry):
        for h in range(2):
            for way in range(2):
                at = z - t if way == 0 else z + t
                there = jnp.logical_and(jnp.logical_and(at >= 0, at < nz), t > 0)
                origin = jnp.clip(at, 0, nz - 1) * 2 + y

                @pl.when(there)
                def _():
                    half_arrived(origin, h)
                    relay_copy(xg.at[origin], origin, t, h, way + 2).start()
                    pl.when(inner[way])(relay_copy(xg.at[origin], origin, t, h, way).start)

        def add_one(k, carry):
            across = k // 2
            away = t - across
            at = jnp.where(lax.rem(k, 2) == 0, z - away, z + away)
            there = jnp.logical_and(at >= 0, at < nz)
            there = jnp.logical_and(there, jnp.logical_and(away >= 0, away < nz))
            there = jnp.logical_and(there, jnp.logical_or(away > 0, lax.rem(k, 2) == 0))
            origin = jnp.clip(at, 0, nz - 1) * 2 + jnp.where(across == 0, y, oy)

            @pl.when(there)
            def _():
                @pl.when(across == 1)
                def _():
                    half_arrived(origin, 0)
                    half_arrived(origin, 1)

                add_block(origin)

            return carry

        return lax.fori_loop(0, 4, add_one, carry)

    lax.fori_loop(0, nz + 1, gather_step, 0)

    mate = chip * 2 + oc
    before = len(pending)
    for i in range(chips):
        to = lax.rem(chip + 1 + i, chips)
        zsend[to] = acc[pl.ds((to * 2 + oc) * rows, rows), :].astype(BF16)
        send(zsend.at[to], s1_recv.at[to], s1_sems.at[0, to], s1_sems.at[1, to], blk, mate)
    total = None
    for i in range(chips):
        to = lax.rem(chip + 1 + i, chips)
        arrived(s1_recv.at[to], s1_sems.at[0, 0], s1_sems.at[1, to])
        part = acc[pl.ds((to * 2 + core) * rows, rows), :] + s1_recv[to].astype(F32)
        if i < chips - 1:
            ysend[to] = part.astype(BF16)
            send(
                ysend.at[to],
                s2_recv.at[chip],
                s2_sems.at[0, to],
                s2_sems.at[1, chip],
                blk,
                to * 2 + core,
            )
        else:
            total = part
    for i in range(chips - 1):
        frm = lax.rem(chip + 1 + i, chips)
        arrived(s2_recv.at[frm], s2_sems.at[0, 0], s2_sems.at[1, frm])
        total = total + s2_recv[frm].astype(F32)
    agg = total.astype(BF16)
    rep_sends = len(pending)

    zvals = zself[...] + dot_nn(agg, wn_ref[...])
    sig = jax.nn.sigmoid(zvals)
    out_ref[...] = (zvals * sig).astype(BF16)
    dz = (cot_ref[...].astype(F32) * sig * (1.0 + zvals * (1.0 - sig))).astype(BF16)
    fhalf = width // 2

    def pass_dg(q, h, at, to):
        half_of = dg.at[q, pl.ds(h * fhalf, fhalf)]
        send(half_of, half_of, dg_ssem.at[at, h], dg_rsem.at[q, h], blk, to)

    def dg_arrived(q, h):
        arrived(dg.at[q, pl.ds(h * fhalf, fhalf)], dg_ssem.at[0, 0], dg_rsem.at[q, h])

    for h in range(2):
        at = slice(h * fhalf, (h + 1) * fhalf)
        dg[rep, at, :] = dot_nt(wn_ref[at, :], dz).astype(BF16)
        for i in range(chips - 1):
            pass_dg(rep, h, i, lax.rem(chip + 1 + i, chips) * 2 + core)
        pass_dg(rep, h, chips, mate)

    gown[0] = dot_tn(x_ref[...], dz)
    gown[1] = dot_tn(agg, dz)
    gbias = jnp.broadcast_to(jnp.sum(dz.astype(F32), axis=0, keepdims=True), (PAD, width))
    ga_send[0:width, :] = gown[oc].astype(BF16)
    ga_send[width : width + PAD, :] = gbias.astype(BF16)
    send(ga_send, ga_recv, ga_sems.at[0], ga_sems.at[1], blk, mate)
    own = dot_nt(dz, ws_ref[...])
    piece = width // nblk

    def pass_chips_dg(h):
        for i in range(chips - 1):
            frm = lax.rem(chip + 1 + i, chips) * 2 + core
            dg_arrived(frm, h)
            pass_dg(frm, h, chips + 1 + i, mate)

    pass_chips_dg(0)

    arrived(ga_recv, ga_sems.at[0], ga_sems.at[1])
    gbias = gbias.astype(BF16).astype(F32) + ga_recv[width : width + PAD, :].astype(F32)
    gown[0] = gown[core] + ga_recv[0:width, :].astype(F32)
    for b in range(nblk):
        gc_send[b, 0:piece, :] = gown[0, b * piece : (b + 1) * piece].astype(BF16)
        gc_send[b, piece : piece + PAD, :] = gbias.astype(BF16)
    gc_buf[blk] = gc_send[blk]
    for i in range(1, nblk):
        to = lax.rem(blk + i, nblk)
        send(gc_send.at[to], gc_buf.at[blk], gc_sems.at[0, to], gc_sems.at[1, blk], to, rep)

    pass_chips_dg(1)

    for _, copy in pending[before:rep_sends]:
        copy.wait_send()
    del pending[before:rep_sends]

    def term(c, lo=0, count=width):
        if nrep <= 4:
            out = dot_nn(dg[0, lo : lo + count], dense[c, 0:rows, :])
            for q in range(1, nrep):
                out = out + dot_nn(
                    dg[q, lo : lo + count], dense[c, q * rows : (q + 1) * rows, :]
                )
            return out

        def step(q, out):
            return out + dot_nn(dg[q, lo : lo + count], dense[c, pl.ds(q * rows, rows), :])

        return lax.fori_loop(0, nrep, step, jnp.zeros((count, rows), F32))

    def y_copy(dest, h):
        at = pl.ds(h * fhalf, fhalf)
        return pltpu.make_async_remote_copy(
            src_ref=ysend.at[dest, at],
            dst_ref=yrecv.at[dest, at],
            send_sem=y_sems.at[0, dest, h],
            recv_sem=y_sems.at[1, dest, h],
            device_id=(z * 2 + oy, rep),
            device_id_type=MESH,
        )

    def grad_blocks():
        for i in range(1, nblk):
            frm = lax.rem(blk + i, nblk)
            arrived(gc_buf.at[frm], gc_sems.at[0, 0], gc_sems.at[1, frm])
        tot = gc_buf[0].astype(F32)
        for b in range(1, nblk):
            tot = tot + gc_buf[b].astype(F32)
        gb_buf[chip] = tot.astype(BF16)
        for i in range(chips - 1):
            to = lax.rem(chip + 1 + i, chips)
            send(
                gb_buf.at[chip],
                gb_buf.at[chip],
                gb_sems.at[0, i],
                gb_sems.at[1, chip],
                blk,
                to * 2 + core,
            )

    def grad_chips():
        for i in range(chips - 1):
            frm = lax.rem(chip + 1 + i, chips)
            arrived(gb_buf.at[frm], gb_sems.at[0, 0], gb_sems.at[1, frm])
        tot = gb_buf[0].astype(F32)
        for i in range(1, chips):
            tot = tot + gb_buf[i].astype(F32)
        gb_ref[...] = tot[piece : piece + 1]
        here = ge_buf.at[core, pl.ds(blk * piece, piece)]
        ge_buf[core, pl.ds(blk * piece, piece), :] = tot[0:piece].astype(BF16)
        for i in range(1, nblk):
            to = lax.rem(blk + i, nblk)
            send(here, here, gd_sems.at[0, to], gd_sems.at[1, blk], to, rep)

    near = jnp.minimum(z, nz - 1 - z)

    def y_dest(i):
        dest = jnp.where(
            i < 2 * near,
            jnp.where(lax.rem(i, 2) == 0, nz - 1 - i // 2, i // 2),
            nz - 1 - (i - near),
        )
        return jnp.where(z < nz // 2, dest, nz - 1 - dest)

    def send_y(i, carry):
        dest = y_dest(i)
        ysend[dest] = term(dest * 2 + oy).astype(BF16)
        y_copy(dest, 0).start()
        y_copy(dest, 1).start()
        return carry

    for h in range(2):
        for i in range(chips):
            dg_arrived(lax.rem(chip + i, chips) * 2 + oc, h)
    lax.fori_loop(0, nz, send_y, 0)
    grad_blocks()

    def own_term(i, carry):
        acc[pl.ds(i * width, width), :] = term(i * 2 + y)
        return carry

    lax.fori_loop(0, nz, own_term, 0)

    def grad_back():
        for i in range(1, nblk):
            frm = lax.rem(blk + i, nblk)
            arrived(
                ge_buf.at[core, pl.ds(frm * piece, piece)], gd_sems.at[0, 0], gd_sems.at[1, frm]
            )
        send(ge_buf.at[core], ge_buf.at[core], gf_sems.at[0], gf_sems.at[1], blk, mate)

    def add_from(buf, dest, h, sem):
        at = pl.ds(dest * width + h * fhalf, fhalf)
        arrived(buf.at[pl.ds(h * fhalf, fhalf)], z_ssem.at[0, 0], sem)
        acc[at, :] += buf[h * fhalf : (h + 1) * fhalf, :].astype(F32)

    def chain_at(j):
        way = jnp.where(z < nz // 2, lax.rem(j, 2), 1 - lax.rem(j, 2))
        dest = jnp.where(way == 0, nz - 1 - j // 2, j // 2)
        on = jnp.where(way == 0, blk + 2, blk - 2)
        cond = jnp.where(way == 0, z < dest, z > dest)
        more = jnp.where(way == 0, z > 0, z < nz - 1)

        def copy(h):
            at = pl.ds(h * fhalf, fhalf)
            return pltpu.make_async_remote_copy(
                src_ref=zsend.at[dest, at],
                dst_ref=zrecv.at[way, dest, at],
                send_sem=z_ssem.at[dest, h],
                recv_sem=z_rsem.at[way, dest, h],
                device_id=(on, rep),
                device_id_type=MESH,
            )

        return way, dest, cond, more, copy

    def chain(j, carry):
        way, dest, cond, more, copy = chain_at(j)

        @pl.when(cond)
        def _():
            for h in range(2):
                add_from(yrecv.at[dest], dest, h, y_sems.at[1, dest, h])

                @pl.when(more)
                def _():
                    add_from(zrecv.at[way, dest], dest, h, z_rsem.at[way, dest, h])

                rows_at = pl.ds(dest * width + h * fhalf, fhalf)
                zsend[dest, h * fhalf : (h + 1) * fhalf, :] = acc[rows_at, :].astype(BF16)
                copy(h).start()

        return carry

    grad_chips()
    lax.fori_loop(0, 2 * (nz - 1), chain, 0)

    grad_back()
    for h in range(2):
        add_from(yrecv.at[z], z, h, y_sems.at[1, z, h])

        @pl.when(z > 0)
        def _():
            add_from(zrecv.at[0, z], z, h, z_rsem.at[0, z, h])

        @pl.when(z < nz - 1)
        def _():
            add_from(zrecv.at[1, z], z, h, z_rsem.at[1, z, h])

    gradf_ref[...] = (own + acc[pl.ds(z * width, width), :].T).astype(BF16)

    arrived(ge_buf.at[oc], gf_sems.at[0], gf_sems.at[1])
    ge_ref[...] = ge_buf[...]

    for cond, copy in pending:
        if cond is None:
            copy.wait_send()
        else:
            pl.when(cond)(copy.wait_send)

    def drain_y(i, carry):
        y_copy(i, 0).wait_send()
        y_copy(i, 1).wait_send()
        return carry

    lax.fori_loop(0, nz, drain_y, 0)

    def drain_chain(j, carry):
        _, _, cond, _, copy = chain_at(j)

        @pl.when(cond)
        def _():
            copy(0).wait_send()
            copy(1).wait_send()

        return carry

    lax.fori_loop(0, 2 * (nz - 1), drain_chain, 0)

    def drain_relay(t, carry):
        for way in range(2):
            at = z - t if way == 0 else z + t
            there = jnp.logical_and(at >= 0, at < nz)
            origin = jnp.clip(at, 0, nz - 1) * 2 + y
            for h in range(2):
                onward = relay_copy(xg.at[origin], origin, t, h, way)
                pl.when(jnp.logical_and(there, inner[way]))(onward.wait_send)
                over = relay_copy(xg.at[origin], origin, t, h, way + 2)
                if way == 0:
                    pl.when(there)(over.wait_send)
                else:
                    pl.when(jnp.logical_and(there, t > 0))(over.wait_send)
        return carry

    lax.fori_loop(0, nz, drain_relay, 0)


def hand_out(a_ref, b_ref, c_ref, d_ref, out_ref, gradf_ref, gs_ref, gn_ref, gb_ref):
    out_ref[...] = a_ref[...]
    gradf_ref[...] = b_ref[...]
    gs_ref[...] = c_ref[0].astype(F32)
    gn_ref[...] = c_ref[1].astype(F32)
    gb_ref[...] = d_ref[...]


def local(
    features, w_self, w_neigh, bias, cotangent, tile_values, tile_rows, tile_cols, tile_counts
):
    rows, width = features.shape
    nblk, nrep = lax.axis_size("blk"), lax.axis_size("rep")
    slots, tile = tile_values.shape[3], tile_values.shape[4]
    per_dev = rows // tile
    lanes = max(128, nrep * per_dev * per_dev)
    nz, chips = nblk // 2, nrep // 2
    piece = width // nblk

    cfg = (nblk, nrep, slots, tile, rows, width)
    vmem = pl.BlockSpec(memory_space=pltpu.VMEM)
    sems = pltpu.SemaphoreType.DMA
    outs = pl.pallas_call(
        functools.partial(kernel, cfg),
        out_shape=(
            jax.ShapeDtypeStruct((rows, width), BF16),
            jax.ShapeDtypeStruct((rows, width), BF16),
            jax.ShapeDtypeStruct((2, width, width), BF16),
            jax.ShapeDtypeStruct((1, width), F32),
        ),
        in_specs=[
            pl.BlockSpec(memory_space=pltpu.SMEM),
            vmem,
            vmem,
            vmem,
            vmem,
            vmem,
            vmem,
            vmem,
            pl.BlockSpec(memory_space=pl.ANY),
        ],
        out_specs=(vmem,) * 4,
        scratch_shapes=[
            pltpu.VMEM((nblk * slots + 1, tile, tile), BF16),
            pltpu.VMEM((nblk, nrep * rows, rows), BF16),
            pltpu.VMEM((nblk, rows, width), BF16),
            pltpu.VMEM((max(nrep * rows, nz * width), width), F32),
            pltpu.VMEM((rows, width), F32),
            pltpu.VMEM((max(chips, nz), rows, width), BF16),
            pltpu.VMEM((chips, rows, width), BF16),
            pltpu.VMEM((max(chips, nz), rows, width), BF16),
            pltpu.VMEM((chips, rows, width), BF16),
            pltpu.VMEM((nrep, width, rows), BF16),
                pltpu.VMEM((nz, width, rows), BF16),
            pltpu.VMEM((2, nz, width, rows), BF16),
            pltpu.VMEM((2, width, width), F32),
            pltpu.VMEM((width + PAD, width), BF16),
            pltpu.VMEM((width + PAD, width), BF16),
            pltpu.VMEM((chips, piece + PAD, width), BF16),
            pltpu.VMEM((nblk, piece + PAD, width), BF16),
            pltpu.VMEM((nblk, piece + PAD, width), BF16),
            pltpu.VMEM((2, width, width), BF16),
            pltpu.VMEM((nblk, lanes), jnp.int32),
            pltpu.SMEM((nblk, lanes), jnp.int32),
            sems,
            sems,
            sems((nblk, 2)),
            sems((nz, 2, 4)),
            sems((2, chips)),
            sems((2, chips)),
            sems((nrep, 2)),
            sems((2 * chips + 1, 2)),
            sems((2, nz, 2)),
            sems((nz, 2)),
            sems((2, nz, 2)),
            sems((2,)),
            sems((2, chips)),
            sems((2, nblk)),
            sems((2, nblk)),
            sems((2,)),
        ],
        compiler_params=pltpu.CompilerParams(
            collective_id=0, has_side_effects=True, vmem_limit_bytes=60 * 1024 * 1024
        ),
        cost_estimate=pl.CostEstimate(
            flops=4 * nblk * nrep * rows * rows * width,
            bytes_accessed=nblk * slots * tile * tile * 2,
            transcendentals=rows * width,
        ),
    )(
        tile_counts.reshape(1, nblk),
        tile_rows.reshape(nblk, slots),
        tile_cols.reshape(nblk, slots),
        features,
        w_self,
        w_neigh,
        bias.reshape(1, width),
        cotangent,
        tile_values.reshape(nblk * slots, tile, tile),
    )
    output, grad_features, grad_self, grad_neigh, grad_bias = pl.pallas_call(
        hand_out,
        out_shape=(
            jax.ShapeDtypeStruct((rows, width), BF16),
            jax.ShapeDtypeStruct((rows, width), BF16),
            jax.ShapeDtypeStruct((width, width), F32),
            jax.ShapeDtypeStruct((width, width), F32),
            jax.ShapeDtypeStruct((1, width), F32),
        ),
        in_specs=[vmem] * 4,
        out_specs=(vmem,) * 5,
    )(*outs)
    return output, grad_features, grad_self, grad_neigh, grad_bias.reshape(width)


def solution(mesh):
    in_specs = (
        P(("blk", "rep"), None),
        P(),
        P(),
        P(),
        P(("blk", "rep"), None),
        P("blk", "rep", None, None, None, None),
        P("blk", "rep", None, None),
        P("blk", "rep", None, None),
        P("blk", "rep", None),
    )
    out_specs = (P(("blk", "rep"), None), P(("blk", "rep"), None), P(), P(), P())
    return jax.shard_map(local, mesh=mesh, in_specs=in_specs, out_specs=out_specs, check_vma=False)
```

```python
import functools

import jax
import jax.numpy as jnp
from jax import lax
from jax.experimental import pallas as pl
from jax.experimental.pallas import tpu as pltpu
from jax.sharding import PartitionSpec as P

MESH = pl.DeviceIdType.MESH
F32 = jnp.float32
BF16 = jnp.bfloat16
PAD = 16


def dot_nn(a, b):
    return jnp.dot(a, b, preferred_element_type=F32)


def dot_nt(a, b):
    return lax.dot_general(a, b, (((1,), (1,)), ((), ())), preferred_element_type=F32)


def dot_tn(a, b):
    return lax.dot_general(a, b, (((0,), (0,)), ((), ())), preferred_element_type=F32)


def kernel(
    cfg,
    counts_ref,
    trows_ref,
    tcols_ref,
    x_ref,
    ws_ref,
    wn_ref,
    bias_ref,
    cot_ref,
    values_ref,
    out_ref,
    gradf_ref,
    ge_ref,
    gb_ref,
    vals,
    dense,
    xg,
    acc,
    zself,
    zsend,
    s1_recv,
    ysend,
    s2_recv,
    dg,
    yrecv,
    zrecv,
    gown,
    ga_send,
    ga_recv,
    gb_buf,
    gc_buf,
    gc_send,
    ge_buf,
    place_vec,
    place_ref,
    vals_sem,
    place_sem,
    x_rsem,
    x_ssem,
    s1_sems,
    s2_sems,
    dg_rsem,
    dg_ssem,
    y_sems,
    z_ssem,
    z_rsem,
    ga_sems,
    gb_sems,
    gc_sems,
    gd_sems,
    gf_sems,
):
    nblk, nrep, slots, tile, rows, width = cfg
    nz, chips = nblk // 2, nrep // 2
    per_dev = rows // tile
    rtiles = nrep * per_dev
    blk = lax.axis_index("blk")
    rep = lax.axis_index("rep")
    z, y = blk // 2, lax.rem(blk, 2)
    chip, core = rep // 2, lax.rem(rep, 2)
    oy, oc = 1 - y, 1 - core

    pending = []

    def send(src, dst, ssem, rsem, to_blk, to_rep, cond=None):
        copy = pltpu.make_async_remote_copy(
            src_ref=src,
            dst_ref=dst,
            send_sem=ssem,
            recv_sem=rsem,
            device_id=(to_blk, to_rep),
            device_id_type=MESH,
        )
        if cond is None:
            copy.start()
        else:
            pl.when(cond)(copy.start)
        pending.append((cond, copy))

    def arrived(dst, ssem, rsem):
        pltpu.make_async_remote_copy(
            src_ref=dst,
            dst_ref=dst,
            send_sem=ssem,
            recv_sem=rsem,
            device_id=(blk, rep),
            device_id_type=MESH,
        ).wait_recv()

    load = pltpu.make_async_copy(values_ref, vals.at[pl.ds(0, nblk * slots)], vals_sem)
    load.start()

    lanes = place_vec.shape[1]
    row_at = lax.broadcasted_iota(jnp.int32, (nblk, lanes), 0)
    lane = lax.broadcasted_iota(jnp.int32, (nblk, lanes), 1)

    def find_places():
        live = jnp.zeros((nblk, lanes), jnp.int32)
        for c in range(nblk):
            live = jnp.where(row_at == c, counts_ref[0, c], live)
        at = trows_ref[...] * per_dev + tcols_ref[...]
        found = jnp.full((nblk, lanes), nblk * slots, jnp.int32)
        for slot in range(slots):
            hit = jnp.logical_and(at[:, slot : slot + 1] == lane, live > slot)
            found = jnp.where(hit, row_at * slots + slot, found)
        place_vec[...] = found
        move = pltpu.make_async_copy(place_vec, place_ref, place_sem)
        move.start()
        return move

    barrier = pltpu.get_barrier_semaphore()
    for i in range(1, nblk):
        pl.semaphore_signal(
            barrier, inc=1, device_id=(lax.rem(blk + i, nblk), rep), device_id_type=MESH
        )
    for i in range(1, nrep):
        pl.semaphore_signal(
            barrier, inc=1, device_id=(blk, lax.rem(rep + i, nrep)), device_id_type=MESH
        )
    pl.semaphore_wait(barrier, nblk + nrep - 2)

    part = rows // 4

    def pass_on(src, origin, step, h, kind, to_blk, cond):
        send(
            src.at[pl.ds(h * part, part)],
            xg.at[origin, pl.ds(h * part, part)],
            x_ssem.at[step, h, kind],
            x_rsem.at[origin, h],
            to_blk,
            rep,
            cond,
        )

    def part_arrived(origin, h):
        arrived(xg.at[origin, pl.ds(h * part, part)], x_ssem.at[0, 0, 0], x_rsem.at[origin, h])

    for h in range(4):
        pass_on(x_ref, blk, 0, h, 0, blk + 2, z < nz - 1)
        pass_on(x_ref, blk, 0, h, 1, blk - 2, z > 0)
        pass_on(x_ref, blk, 0, h, 2, z * 2 + oy, None)
    xg[blk] = x_ref[...]

    move = find_places()
    zself[...] = dot_nn(x_ref[...], ws_ref[...]) + bias_ref[...]
    vals[nblk * slots] = jnp.zeros((tile, tile), BF16)
    move.wait()
    load.wait()

    def place_tiles(c, carry):
        def place_row(r):
            for t in range(per_dev):
                dense[c, pl.ds(r * tile, tile), t * tile : (t + 1) * tile] = vals[
                    place_ref[c, r * per_dev + t]
                ]

        if rtiles <= 8:
            for r in range(rtiles):
                place_row(r)
        else:
            pl.loop(0, rtiles)(place_row)
        return carry

    lax.fori_loop(0, nblk, place_tiles, 0)

    chunk = nrep * rows if nrep <= 4 else rows

    def add_block(c, first=False):
        def part(i):
            at = pl.ds(i * chunk, chunk)
            prod = dot_nn(dense[c, at, :], xg[c])
            if first:
                acc[at, :] = prod
            else:
                acc[at, :] += prod

        count = nrep * rows // chunk
        if count == 1:
            part(0)
        else:
            pl.loop(0, count)(part)

    add_block(blk, True)

    def add_pair(step, side, wait):
        for at in (z - step, z + step):
            origin = at * 2 + side

            @pl.when(jnp.logical_and(at >= 0, at < nz))
            def _():
                if wait:
                    for h in range(4):
                        part_arrived(origin, h)
                add_block(origin)

    for t in range(1, nz):
        for h in range(4):
            for at, kind, inner in ((z - t, 0, z < nz - 1), (z + t, 1, z > 0)):
                origin = at * 2 + y
                there = at >= 0 if kind == 0 else at < nz
                on = blk + 2 if kind == 0 else blk - 2

                @pl.when(there)
                def _():
                    part_arrived(origin, h)

                held = xg.at[origin]
                pass_on(held, origin, t, h, kind, on, jnp.logical_and(there, inner))
                pass_on(held, origin, t, h, kind + 2, z * 2 + oy, there)
        add_pair(t, y, False)
        if t == 1:
            for h in range(4):
                part_arrived(z * 2 + oy, h)
            add_block(z * 2 + oy)
        else:
            add_pair(t - 1, oy, True)
    add_pair(nz - 1, oy, True)

    mate = chip * 2 + oc
    before = len(pending)
    for i in range(chips):
        to = lax.rem(chip + 1 + i, chips)
        zsend[to] = acc[pl.ds((to * 2 + oc) * rows, rows), :].astype(BF16)
        send(zsend.at[to], s1_recv.at[to], s1_sems.at[0, to], s1_sems.at[1, to], blk, mate)
    total = None
    for i in range(chips):
        to = lax.rem(chip + 1 + i, chips)
        arrived(s1_recv.at[to], s1_sems.at[0, 0], s1_sems.at[1, to])
        part = acc[pl.ds((to * 2 + core) * rows, rows), :] + s1_recv[to].astype(F32)
        if i < chips - 1:
            ysend[to] = part.astype(BF16)
            send(
                ysend.at[to],
                s2_recv.at[chip],
                s2_sems.at[0, to],
                s2_sems.at[1, chip],
                blk,
                to * 2 + core,
            )
        else:
            total = part
    for i in range(chips - 1):
        frm = lax.rem(chip + 1 + i, chips)
        arrived(s2_recv.at[frm], s2_sems.at[0, 0], s2_sems.at[1, frm])
        total = total + s2_recv[frm].astype(F32)
    agg = total.astype(BF16)
    rep_sends = len(pending)

    zvals = zself[...] + dot_nn(agg, wn_ref[...])
    sig = jax.nn.sigmoid(zvals)
    out_ref[...] = (zvals * sig).astype(BF16)
    dz = (cot_ref[...].astype(F32) * sig * (1.0 + zvals * (1.0 - sig))).astype(BF16)
    fhalf = width // 2

    def pass_dg(q, h, at, to):
        half_of = dg.at[q, pl.ds(h * fhalf, fhalf)]
        send(half_of, half_of, dg_ssem.at[at, h], dg_rsem.at[q, h], blk, to)

    def dg_arrived(q, h):
        arrived(dg.at[q, pl.ds(h * fhalf, fhalf)], dg_ssem.at[0, 0], dg_rsem.at[q, h])

    for h in range(2):
        at = slice(h * fhalf, (h + 1) * fhalf)
        dg[rep, at, :] = dot_nt(wn_ref[at, :], dz).astype(BF16)
        for i in range(chips - 1):
            pass_dg(rep, h, i, lax.rem(chip + 1 + i, chips) * 2 + core)
        pass_dg(rep, h, chips, mate)

    gown[0] = dot_tn(x_ref[...], dz)
    gown[1] = dot_tn(agg, dz)
    gbias = jnp.broadcast_to(jnp.sum(dz.astype(F32), axis=0, keepdims=True), (PAD, width))
    ga_send[0:width, :] = gown[oc].astype(BF16)
    ga_send[width : width + PAD, :] = gbias.astype(BF16)
    send(ga_send, ga_recv, ga_sems.at[0], ga_sems.at[1], blk, mate)
    own = dot_nt(dz, ws_ref[...])
    piece = width // nblk

    def pass_chips_dg(h):
        for i in range(chips - 1):
            frm = lax.rem(chip + 1 + i, chips) * 2 + core
            dg_arrived(frm, h)
            pass_dg(frm, h, chips + 1 + i, mate)

    pass_chips_dg(0)

    arrived(ga_recv, ga_sems.at[0], ga_sems.at[1])
    gbias = gbias.astype(BF16).astype(F32) + ga_recv[width : width + PAD, :].astype(F32)
    gown[0] = gown[core] + ga_recv[0:width, :].astype(F32)
    for b in range(nblk):
        gc_send[b, 0:piece, :] = gown[0, b * piece : (b + 1) * piece].astype(BF16)
        gc_send[b, piece : piece + PAD, :] = gbias.astype(BF16)
    gc_buf[blk] = gc_send[blk]
    for i in range(1, nblk):
        to = lax.rem(blk + i, nblk)
        send(gc_send.at[to], gc_buf.at[blk], gc_sems.at[0, to], gc_sems.at[1, blk], to, rep)

    pass_chips_dg(1)

    for _, copy in pending[before:rep_sends]:
        copy.wait_send()
    del pending[before:rep_sends]

    def term(c, lo=0, count=width):
        if nrep <= 4:
            out = dot_nn(dg[0, lo : lo + count], dense[c, 0:rows, :])
            for q in range(1, nrep):
                out = out + dot_nn(
                    dg[q, lo : lo + count], dense[c, q * rows : (q + 1) * rows, :]
                )
            return out

        def step(q, out):
            return out + dot_nn(dg[q, lo : lo + count], dense[c, pl.ds(q * rows, rows), :])

        return lax.fori_loop(0, nrep, step, jnp.zeros((count, rows), F32))

    def y_copy(dest, h):
        at = pl.ds(h * fhalf, fhalf)
        return pltpu.make_async_remote_copy(
            src_ref=ysend.at[dest, at],
            dst_ref=yrecv.at[dest, at],
            send_sem=y_sems.at[0, dest, h],
            recv_sem=y_sems.at[1, dest, h],
            device_id=(z * 2 + oy, rep),
            device_id_type=MESH,
        )

    def grad_blocks():
        for i in range(1, nblk):
            frm = lax.rem(blk + i, nblk)
            arrived(gc_buf.at[frm], gc_sems.at[0, 0], gc_sems.at[1, frm])
        tot = gc_buf[0].astype(F32)
        for b in range(1, nblk):
            tot = tot + gc_buf[b].astype(F32)
        gb_buf[chip] = tot.astype(BF16)
        for i in range(chips - 1):
            to = lax.rem(chip + 1 + i, chips)
            send(
                gb_buf.at[chip],
                gb_buf.at[chip],
                gb_sems.at[0, i],
                gb_sems.at[1, chip],
                blk,
                to * 2 + core,
            )

    def grad_chips():
        for i in range(chips - 1):
            frm = lax.rem(chip + 1 + i, chips)
            arrived(gb_buf.at[frm], gb_sems.at[0, 0], gb_sems.at[1, frm])
        tot = gb_buf[0].astype(F32)
        for i in range(1, chips):
            tot = tot + gb_buf[i].astype(F32)
        gb_ref[...] = tot[piece : piece + 1]
        here = ge_buf.at[core, pl.ds(blk * piece, piece)]
        ge_buf[core, pl.ds(blk * piece, piece), :] = tot[0:piece].astype(BF16)
        for i in range(1, nblk):
            to = lax.rem(blk + i, nblk)
            send(here, here, gd_sems.at[0, to], gd_sems.at[1, blk], to, rep)

    near = jnp.minimum(z, nz - 1 - z)

    def y_dest(i):
        dest = jnp.where(
            i < 2 * near,
            jnp.where(lax.rem(i, 2) == 0, nz - 1 - i // 2, i // 2),
            nz - 1 - (i - near),
        )
        return jnp.where(z < nz // 2, dest, nz - 1 - dest)

    def send_y(i, carry):
        dest = y_dest(i)
        ysend[dest] = term(dest * 2 + oy).astype(BF16)
        y_copy(dest, 0).start()
        y_copy(dest, 1).start()
        return carry

    far = y_dest(jnp.int32(0))
    for h in range(2):
        for i in range(chips):
            dg_arrived(lax.rem(chip + i, chips) * 2 + oc, h)
        at = slice(h * fhalf, (h + 1) * fhalf)
        ysend[far, at, :] = term(far * 2 + oy, h * fhalf, fhalf).astype(BF16)
        y_copy(far, h).start()
    lax.fori_loop(1, nz, send_y, 0)
    grad_blocks()

    def own_term(i, carry):
        acc[pl.ds(i * width, width), :] = term(i * 2 + y)
        return carry

    lax.fori_loop(0, nz, own_term, 0)

    def grad_back():
        for i in range(1, nblk):
            frm = lax.rem(blk + i, nblk)
            arrived(
                ge_buf.at[core, pl.ds(frm * piece, piece)], gd_sems.at[0, 0], gd_sems.at[1, frm]
            )
        send(ge_buf.at[core], ge_buf.at[core], gf_sems.at[0], gf_sems.at[1], blk, mate)

    def add_from(buf, dest, h, sem):
        at = pl.ds(dest * width + h * fhalf, fhalf)
        arrived(buf.at[pl.ds(h * fhalf, fhalf)], z_ssem.at[0, 0], sem)
        acc[at, :] += buf[h * fhalf : (h + 1) * fhalf, :].astype(F32)

    def chain(k, way, cond):
        dest = nz - 1 - k if way == 0 else k
        on = blk + 2 if way == 0 else blk - 2
        more = z > 0 if way == 0 else z < nz - 1
        cond = jnp.logical_and(cond, z < dest if way == 0 else z > dest)
        for h in range(2):

            @pl.when(cond)
            def _():
                add_from(yrecv.at[dest], dest, h, y_sems.at[1, dest, h])

                @pl.when(more)
                def _():
                    add_from(zrecv.at[way, dest], dest, h, z_rsem.at[way, dest, h])

                rows_at = pl.ds(dest * width + h * fhalf, fhalf)
                zsend[dest, h * fhalf : (h + 1) * fhalf, :] = acc[rows_at, :].astype(BF16)

            at = pl.ds(h * fhalf, fhalf)
            send(
                zsend.at[dest, at],
                zrecv.at[way, dest, at],
                z_ssem.at[dest, h],
                z_rsem.at[way, dest, h],
                on,
                rep,
                cond,
            )

    at_end = near == 0
    chain(0, 0, z == 0)
    chain(0, 1, z == nz - 1)
    grad_chips()
    for k in range(nz - 1):
        inside = z >= 0 if k else jnp.logical_not(at_end)
        chain(k, 0, jnp.logical_and(inside, z < nz // 2))
        chain(k, 1, inside)
        chain(k, 0, jnp.logical_and(inside, z >= nz // 2))

    grad_back()
    for h in range(2):
        add_from(yrecv.at[z], z, h, y_sems.at[1, z, h])

        @pl.when(z > 0)
        def _():
            add_from(zrecv.at[0, z], z, h, z_rsem.at[0, z, h])

        @pl.when(z < nz - 1)
        def _():
            add_from(zrecv.at[1, z], z, h, z_rsem.at[1, z, h])

    gradf_ref[...] = (own + acc[pl.ds(z * width, width), :].T).astype(BF16)

    arrived(ge_buf.at[oc], gf_sems.at[0], gf_sems.at[1])
    ge_ref[...] = ge_buf[...]

    for cond, copy in pending:
        if cond is None:
            copy.wait_send()
        else:
            pl.when(cond)(copy.wait_send)

    def drain_y(i, carry):
        y_copy(i, 0).wait_send()
        y_copy(i, 1).wait_send()
        return carry

    lax.fori_loop(0, nz, drain_y, 0)


def hand_out(a_ref, b_ref, c_ref, d_ref, out_ref, gradf_ref, gs_ref, gn_ref, gb_ref):
    out_ref[...] = a_ref[...]
    gradf_ref[...] = b_ref[...]
    gs_ref[...] = c_ref[0].astype(F32)
    gn_ref[...] = c_ref[1].astype(F32)
    gb_ref[...] = d_ref[...]


def local(
    features, w_self, w_neigh, bias, cotangent, tile_values, tile_rows, tile_cols, tile_counts
):
    rows, width = features.shape
    nblk, nrep = lax.axis_size("blk"), lax.axis_size("rep")
    slots, tile = tile_values.shape[3], tile_values.shape[4]
    per_dev = rows // tile
    lanes = max(128, nrep * per_dev * per_dev)
    nz, chips = nblk // 2, nrep // 2
    piece = width // nblk

    cfg = (nblk, nrep, slots, tile, rows, width)
    vmem = pl.BlockSpec(memory_space=pltpu.VMEM)
    sems = pltpu.SemaphoreType.DMA
    outs = pl.pallas_call(
        functools.partial(kernel, cfg),
        out_shape=(
            jax.ShapeDtypeStruct((rows, width), BF16),
            jax.ShapeDtypeStruct((rows, width), BF16),
            jax.ShapeDtypeStruct((2, width, width), BF16),
            jax.ShapeDtypeStruct((1, width), F32),
        ),
        in_specs=[
            pl.BlockSpec(memory_space=pltpu.SMEM),
            vmem,
            vmem,
            vmem,
            vmem,
            vmem,
            vmem,
            vmem,
            pl.BlockSpec(memory_space=pl.ANY),
        ],
        out_specs=(vmem,) * 4,
        scratch_shapes=[
            pltpu.VMEM((nblk * slots + 1, tile, tile), BF16),
            pltpu.VMEM((nblk, nrep * rows, rows), BF16),
            pltpu.VMEM((nblk, rows, width), BF16),
            pltpu.VMEM((max(nrep * rows, nz * width), width), F32),
            pltpu.VMEM((rows, width), F32),
            pltpu.VMEM((max(chips, nz), rows, width), BF16),
            pltpu.VMEM((chips, rows, width), BF16),
            pltpu.VMEM((max(chips, nz), rows, width), BF16),
            pltpu.VMEM((chips, rows, width), BF16),
            pltpu.VMEM((nrep, width, rows), BF16),
                pltpu.VMEM((nz, width, rows), BF16),
            pltpu.VMEM((2, nz, width, rows), BF16),
            pltpu.VMEM((2, width, width), F32),
            pltpu.VMEM((width + PAD, width), BF16),
            pltpu.VMEM((width + PAD, width), BF16),
            pltpu.VMEM((chips, piece + PAD, width), BF16),
            pltpu.VMEM((nblk, piece + PAD, width), BF16),
            pltpu.VMEM((nblk, piece + PAD, width), BF16),
            pltpu.VMEM((2, width, width), BF16),
            pltpu.VMEM((nblk, lanes), jnp.int32),
            pltpu.SMEM((nblk, lanes), jnp.int32),
            sems,
            sems,
            sems((nblk, 4)),
            sems((nz, 4, 4)),
            sems((2, chips)),
            sems((2, chips)),
            sems((nrep, 2)),
            sems((2 * chips + 1, 2)),
            sems((2, nz, 2)),
            sems((nz, 2)),
            sems((2, nz, 2)),
            sems((2,)),
            sems((2, chips)),
            sems((2, nblk)),
            sems((2, nblk)),
            sems((2,)),
        ],
        compiler_params=pltpu.CompilerParams(
            collective_id=0, has_side_effects=True, vmem_limit_bytes=60 * 1024 * 1024
        ),
        cost_estimate=pl.CostEstimate(
            flops=4 * nblk * nrep * rows * rows * width,
            bytes_accessed=nblk * slots * tile * tile * 2,
            transcendentals=rows * width,
        ),
    )(
        tile_counts.reshape(1, nblk),
        tile_rows.reshape(nblk, slots),
        tile_cols.reshape(nblk, slots),
        features,
        w_self,
        w_neigh,
        bias.reshape(1, width),
        cotangent,
        tile_values.reshape(nblk * slots, tile, tile),
    )
    output, grad_features, grad_self, grad_neigh, grad_bias = pl.pallas_call(
        hand_out,
        out_shape=(
            jax.ShapeDtypeStruct((rows, width), BF16),
            jax.ShapeDtypeStruct((rows, width), BF16),
            jax.ShapeDtypeStruct((width, width), F32),
            jax.ShapeDtypeStruct((width, width), F32),
            jax.ShapeDtypeStruct((1, width), F32),
        ),
        in_specs=[vmem] * 4,
        out_specs=(vmem,) * 5,
    )(*outs)
    return output, grad_features, grad_self, grad_neigh, grad_bias.reshape(width)


def solution(mesh):
    in_specs = (
        P(("blk", "rep"), None),
        P(),
        P(),
        P(),
        P(("blk", "rep"), None),
        P("blk", "rep", None, None, None, None),
        P("blk", "rep", None, None),
        P("blk", "rep", None, None),
        P("blk", "rep", None),
    )
    out_specs = (P(("blk", "rep"), None), P(("blk", "rep"), None), P(), P(), P())
    return jax.shard_map(local, mesh=mesh, in_specs=in_specs, out_specs=out_specs, check_vma=False)
```
